128 devices in a mesh: ctx: 16 (over z, x), tp: 8 (over y, core).
Axes of the slice: x: 4, y: 4, z: 4, core: 2. Of those that a mesh axis runs over, the one named last changes fastest.
Arguments:
- q_raw: bfloat16 [4096, 5120], P('ctx', 'tp'), may hold values from -300 to 300
- k_raw: bfloat16 [4096, 1024], P('ctx', 'tp'), may hold values from -300 to 300
- values: bfloat16 [4096, 1024], P('ctx', 'tp'), may hold values from -6 to 6
- d_out: bfloat16 [4096, 5120], P('ctx', 'tp'), may hold values from -24 to 24
- q_gain: float32 [5120], P('tp'), may hold values from 0.7 to 2
- k_gain: float32 [1024], P('tp'), may hold values from 0.7 to 2
- span_order: int32 [32], replicated, may hold values from 0 to 31, as said below
Outputs:
- d_q_raw: bfloat16 [4096, 5120], P('ctx', 'tp')
- d_k_raw: bfloat16 [4096, 1024], P('ctx', 'tp')
- d_values: bfloat16 [4096, 1024], P('ctx', 'tp')
- d_q_gain: float32 [5120], P('tp')
- d_k_gain: float32 [1024], P('tp')
The draws below stay inside these ranges and needn't reach their ends.
Inputs may be any that keep to these rules, and one draw needn't show every extreme that they name: `span_order`: each span number appears once; slots 2c and 2c + 1 hold two spans that sum to 31.
All inputs are finite; a program needn't handle non-finite values.
Results may differ from the reference program's by a relative error of at most 0.012.
The reference program's roundings to bfloat16 on the way (of `q_rot`, `k_rot`, `probs_b` and `d_scores_b`) count: a program that leaves them out, or rounds other values in their place, can miss the bound.
Values may be sent and summed in bfloat16 or wider, within the bound.
A program may use at most 64 MiB of HBM per device.

```python
import math
import jax
import jax.numpy as jnp
from jax import lax

D = 5120
QH = 40
KVH = 8
DH = 128
SPAN = 128
SPANS = 32
SEQ = 4096
KVD = 1024
GROUP = 5


def column_scale(key, columns):
    spread = jax.random.uniform(key, (1, columns))
    return 10.0 ** (0.25 * jnp.arange(columns, dtype=jnp.float32)[None, :] / columns + 0.5 * spread)


def draw_span_order(key, part):
    key = jax.random.fold_in(key, 7)
    pair_key, flip_key = jax.random.split(key, 2)
    half_count = SPANS // 2
    pairs = jax.random.permutation(pair_key, half_count).astype(jnp.int32)
    flips = jax.random.randint(flip_key, (half_count,), 0, 2, dtype=jnp.int32)
    mirror = (SPANS - 1 - pairs).astype(jnp.int32)
    first = jnp.where(flips == 1, mirror, pairs)
    second = jnp.where(flips == 1, pairs, mirror)
    return jnp.stack([first, second], axis=1).reshape(SPANS).astype(jnp.int32)


def draw_q_raw(key, part):
    key = jax.random.fold_in(key, 3)
    first_key, second_key, third_key = jax.random.split(key, 3)
    scales = column_scale(third_key, D)
    drawn = jnp.clip(jax.random.normal(first_key, (SEQ, D)), -5.0, 5.0)
    row_scale = 10.0 ** jax.random.uniform(second_key, (SEQ, 1))
    return (drawn * row_scale * scales).astype(jnp.bfloat16)


def draw_k_raw(key, part):
    key = jax.random.fold_in(key, 5)
    first_key, second_key, third_key = jax.random.split(key, 3)
    scales = column_scale(third_key, KVD)
    drawn = jnp.clip(jax.random.normal(first_key, (SEQ, KVD)), -5.0, 5.0)
    row_scale = 10.0 ** jax.random.uniform(second_key, (SEQ, 1))
    return (drawn * row_scale * scales).astype(jnp.bfloat16)


def level_of(stream_key, dims, cuts, least, largest):
    def one(position, blocks):
        draws = jax.random.uniform(jax.random.fold_in(jax.random.fold_in(stream_key, 6), position), (blocks,), jnp.float32, least / len(cuts), largest / len(cuts))
        return jnp.repeat(jnp.exp(draws), dims[position] // blocks).reshape((-1,) + (1,) * (len(dims) - position - 1))

    gain = one(*cuts[0])
    for cut in cuts[1:]:
        gain = gain * one(*cut)
    return gain


def gaussian(rng, dims, width, limit, pieces=(), kind=jnp.bfloat16):
    values = jax.random.normal(rng, dims, jnp.float32) * width
    if len(pieces) > 0:
        values = level_of(rng, dims, pieces, -0.22, 0.18) * values
    return jnp.clip(values, min=-limit, max=limit).astype(kind)


def setup_inputs(seed: int = 0) -> dict:
    arg_keys = jax.random.split(jax.random.key(seed), 8)
    return {
        "q_raw": draw_q_raw(jax.random.fold_in(arg_keys[7], 71), 0),
        "k_raw": draw_k_raw(jax.random.fold_in(arg_keys[7], 71), 0),
        "values": gaussian(arg_keys[2], (SEQ, KVD), 1.0, 6.0, ((0, 16), (1, 8))),
        "d_out": gaussian(arg_keys[3], (SEQ, D), 4.0, 24.0, ((0, 16), (1, 8))),
        "q_gain": jnp.clip(jnp.exp(math.log(2.0) - 1.0498221 * jax.random.uniform(arg_keys[4], (D,), jnp.float32) ** level_of(arg_keys[4], (D,), ((0, 8),), -0.2, 0.2)), 0.7, 2.0),
        "k_gain": jnp.clip(jnp.exp(math.log(2.0) - 1.0498221 * jax.random.uniform(arg_keys[5], (KVD,), jnp.float32) ** level_of(arg_keys[5], (KVD,), ((0, 8),), -0.2, 0.2)), 0.7, 2.0),
        "span_order": draw_span_order(jax.random.fold_in(arg_keys[7], 71), 0),
    }


EPS = 1e-06
THETA = 500000.0

def lookup(entries, slots_in):
    matches = slots_in[:, None] == jnp.arange(entries.shape[0], dtype=jnp.int32)[None, :]
    return lax.optimization_barrier(jnp.sum(jnp.where(matches, entries[None, :], 0), axis=1)).astype(jnp.int32)

def token_positions(span_order, start_row, total_rows):
    row_ids = start_row + jnp.arange(total_rows, dtype=jnp.int32)
    return (lookup(span_order, row_ids // SPAN) * SPAN + row_ids % SPAN).astype(jnp.int32)

def rotate(tensor, positions, direction_sign):
    half_width = tensor.shape[-1] // 2
    frequency = THETA ** (-jnp.arange(half_width, dtype=jnp.float32) / half_width)
    angles = positions.astype(jnp.float32)[:, None] * frequency[None, :]
    cos_part = jnp.cos(angles)[:, None, :]
    sin_part = direction_sign * jnp.sin(angles)[:, None, :]
    leading = tensor[..., :half_width]
    trailing = tensor[..., half_width:]
    return jnp.concatenate([leading * cos_part - trailing * sin_part, trailing * cos_part + leading * sin_part], axis=-1)

def normalize(raw_rows, gain_row, positions, head_count):
    as_float = raw_rows.astype(jnp.float32)
    inverse = lax.rsqrt(lax.optimization_barrier(jnp.sum(as_float * as_float, axis=1)) / raw_rows.shape[1] + EPS)
    scaled = as_float * inverse[:, None]
    rotated = rotate((scaled * gain_row[None, :]).reshape(raw_rows.shape[0], head_count, DH), positions, 1.0)
    return (rotated.astype(jnp.bfloat16), scaled, inverse)

def norm_back(d_rotated, positions, scaled, inverse, gain_row):
    d_normed = rotate(d_rotated, positions, -1.0).reshape(scaled.shape)
    d_gain = lax.optimization_barrier(jnp.sum(d_normed * scaled, axis=0))
    scaled_grad = d_normed * gain_row[None, :]
    inner = lax.optimization_barrier(jnp.sum(scaled_grad * scaled, axis=1, keepdims=True)) / scaled.shape[1]
    d_raw = inverse[:, None] * (scaled_grad - scaled * inner)
    return (d_raw.astype(jnp.bfloat16), d_gain)

def reference(q_raw, k_raw, values, d_out, q_gain, k_gain, span_order):
    positions = token_positions(span_order, 0, SEQ)
    q_rot, q_hat, q_inv = normalize(q_raw, q_gain, positions, QH)
    k_rot, k_hat, k_inv = normalize(k_raw, k_gain, positions, KVH)
    score_scale = DH ** (-0.5)
    allowed = positions[None, :] <= positions[:, None]
    query_groups = jnp.transpose(q_rot.reshape(SEQ, KVH, GROUP, DH), (1, 2, 0, 3))
    grad_groups = jnp.transpose(d_out.reshape(SEQ, KVH, GROUP, DH), (1, 2, 0, 3))
    key_groups = jnp.transpose(k_rot.reshape(SEQ, KVH, DH), (1, 0, 2))
    value_groups = jnp.transpose(values.reshape(SEQ, KVH, DH), (1, 0, 2))

    def one_group(inputs):
        queries, grads_out, key_rows, value_rows = inputs
        d_key = jnp.zeros((SEQ, DH), jnp.float32)
        d_value = jnp.zeros((SEQ, DH), jnp.float32)
        d_queries = []
        for member in range(GROUP):
            scores = jnp.dot(queries[member], key_rows.T, preferred_element_type=jnp.float32) * score_scale
            scores = jnp.where(allowed, scores, -jnp.inf)
            top_score = lax.optimization_barrier(jnp.max(scores, axis=1, keepdims=True))
            log_total = top_score + jnp.log(lax.optimization_barrier(jnp.sum(jnp.exp(scores - top_score), axis=1, keepdims=True)))
            probs = jnp.exp(scores - log_total)
            d_probs = jnp.dot(grads_out[member], value_rows.T, preferred_element_type=jnp.float32)
            row_delta = lax.optimization_barrier(jnp.sum(probs * d_probs, axis=1, keepdims=True))
            d_scores = probs * (d_probs - row_delta)
            probs_b = probs.astype(jnp.bfloat16)
            d_scores_b = d_scores.astype(jnp.bfloat16)
            d_queries.append(jnp.dot(d_scores_b, key_rows, preferred_element_type=jnp.float32) * score_scale)
            d_key = d_key + jnp.dot(d_scores_b.T, queries[member], preferred_element_type=jnp.float32) * score_scale
            d_value = d_value + jnp.dot(probs_b.T, grads_out[member], preferred_element_type=jnp.float32)
        return (jnp.stack(d_queries), d_key, d_value)
    d_query_groups, d_key_groups, d_value_groups = lax.map(one_group, (query_groups, grad_groups, key_groups, value_groups))
    d_q_rot = jnp.transpose(d_query_groups, (2, 0, 1, 3)).reshape(SEQ, QH, DH)
    d_k_rot = jnp.transpose(d_key_groups, (1, 0, 2))
    d_values = jnp.transpose(d_value_groups, (1, 0, 2)).reshape(SEQ, KVD).astype(jnp.bfloat16)
    d_q_raw, d_q_gain = norm_back(d_q_rot, positions, q_hat, q_inv, q_gain)
    d_k_raw, d_k_gain = norm_back(d_k_rot, positions, k_hat, k_inv, k_gain)
    return (d_q_raw, d_k_raw, d_values, d_q_gain, d_k_gain)
```

```python
import functools
import math

import jax
import jax.numpy as jnp
import numpy as np
from jax import lax
from jax.experimental import pallas as pl
from jax.experimental.pallas import tpu as pltpu
from jax.sharding import PartitionSpec as P

D = 5120
KVD = 1024
DH = 128
SPAN = 128
SPANS = 32
GROUP = 5
QW = GROUP * DH
EPS = 1e-06
THETA = 500000.0
NEG = -1e30
SCALE = DH ** (-0.5)
C2 = SCALE * math.log2(math.e)
RING = 4
SLOTS = 16
F32 = jnp.float32
BF16 = jnp.bfloat16

ORDER = [
    (0, 0), (0, 3), (3, 0), (0, 1), (1, 0), (3, 3), (1, 3), (3, 1),
    (1, 1), (0, 2), (2, 0), (3, 2), (2, 3), (1, 2), (2, 1), (2, 2),
]
SLOT = {pair: number for number, pair in enumerate(ORDER)}
CHUNKS = ((0, 256), (256, 256), (512, 128))
LOW, HIGH = 0, 1
KEY, VAL = 0, 1


def primary_view(half, slot):
    oz, ox = ORDER[slot]
    return (ox, oz) if half == LOW else (oz, ox)


def slot_of(half, first, second):
    return SLOT[(second, first)] if half == LOW else SLOT[(first, second)]


def gather_sends(half, slot):
    first, second = primary_view(half, slot)
    sends = []
    if second == 0:
        if first == 0:
            sends += [(0, 1, slot_of(half, 3, 0)), (0, 3, slot_of(half, 1, 0))]
        if first == 3:
            sends += [(0, 1, slot_of(half, 2, 0))]
        sends += [(1, 1, slot_of(half, first, 3)), (1, 3, slot_of(half, first, 1))]
    if second == 3:
        sends += [(1, 1, slot_of(half, first, 2))]
    return sends


def tables():
    freq = np.asarray(
        np.float32(THETA) ** (-np.arange(DH // 2, dtype=np.float32) / np.float32(DH // 2)),
        np.float64,
    )
    sign = np.concatenate([-np.ones(DH // 2), np.ones(DH // 2)])

    def pair(numbers):
        angle = np.asarray(numbers, np.float64)[:, None] * freq[None, :]
        cos = np.concatenate([np.cos(angle)] * 2, axis=1)
        sin = np.concatenate([np.sin(angle)] * 2, axis=1) * sign
        return cos, sin

    cos_t, sin_t = pair(np.arange(SPAN))
    cos_s, sin_s = pair(np.arange(SPANS) * SPAN)
    token = np.stack([cos_t, sin_t]).astype(np.float32)
    span = np.stack([cos_s, sin_s])[:, :, None, :].astype(np.float32)
    return jnp.asarray(token), jnp.asarray(span)


def kernel(
    so_ref, q_ref, k_ref, v_ref, do_ref, qg_ref, kg_ref, tab_ref, span_ref,
    dq_out, dk_out, dv_out, dqg_out, dkg_out,
    sel_ref, kv, qs, qt, dos, dot_, rope, qi, ki,
    e_a, e_b, dp_a, dp_b, mh, lh, dh, ml, ll, dl, fh, fl, delta,
    pb, dsb, acc, cb, stage, gotr, pstage, gotp, sg, dkn,
    stat, gain_buf,
    ag_ssem, ag_rsem, rs_ssem, rs_rsem, ps_ssem, ps_rsem,
    st_ssem, st_rsem, gn_ssem, gn_rsem,
):
    ctx = lax.axis_index("ctx")
    tp = lax.axis_index("tp")
    z, x = ctx // RING, ctx % RING
    flip = tp % 2

    def at_offset(oz, ox):
        nz = (z + jnp.where(flip == 0, oz, RING - oz)) % RING
        nx = (x + jnp.where(flip == 0, ox, RING - ox)) % RING
        return nz * RING + nx

    def tp_peer(offset):
        return (tp + offset) % 8

    barrier = pltpu.get_barrier_semaphore()
    for slot in range(1, SLOTS):
        pl.semaphore_signal(
            barrier, inc=1, device_id={"ctx": at_offset(*ORDER[slot])},
            device_id_type=pl.DeviceIdType.MESH,
        )
    for offset in range(1, 8):
        pl.semaphore_signal(
            barrier, inc=1, device_id={"tp": tp_peer(offset)},
            device_id_type=pl.DeviceIdType.MESH,
        )

    s0, s1 = so_ref[2 * ctx], so_ref[2 * ctx + 1]
    low = jnp.minimum(s0, s1)
    spans = (low, SPANS - 1 - low)
    offs = (jnp.where(s0 < s1, 0, 1), jnp.where(s0 < s1, 1, 0))
    for slot in range(1, SLOTS):
        other = at_offset(*ORDER[slot])
        a = jnp.minimum(so_ref[2 * other], so_ref[2 * other + 1])
        sel_ref[slot] = jnp.where(a < low, 1, 0)

    for half in (LOW, HIGH):
        kv[VAL, half, 0] = v_ref[offs[half]]

    pl.semaphore_wait(barrier, 22)

    axis_of = {LOW: ("x", "z"), HIGH: ("z", "x")}

    def neighbour(half, axis, step):
        name = axis_of[half][axis]
        return at_offset(step, 0) if name == "z" else at_offset(0, step)

    def gather_copy(which, half, slot, axis, step, dst):
        return pltpu.make_async_remote_copy(
            src_ref=kv.at[which, half, slot],
            dst_ref=kv.at[which, half, dst],
            send_sem=ag_ssem.at[which, half, dst],
            recv_sem=ag_rsem.at[which, half, dst],
            device_id={"ctx": neighbour(half, axis, step)},
            device_id_type=pl.DeviceIdType.MESH,
        )

    def gather_wait(which, half, slot):
        gather_copy(which, half, slot, 0, 1, slot).wait_recv()

    def gather_forward(which, half, slot):
        for axis, step, dst in gather_sends(half, slot):
            gather_copy(which, half, slot, axis, step, dst).start()

    def hop(which, slots):
        for slot in slots:
            for half in (LOW, HIGH):
                gather_wait(which, half, slot)
                gather_forward(which, half, slot)

    gather_forward(VAL, LOW, 0)
    gather_forward(VAL, HIGH, 0)

    def stat_copy(kind, offset):
        return pltpu.make_async_remote_copy(
            src_ref=stat.at[kind, 0],
            dst_ref=stat.at[kind, offset],
            send_sem=st_ssem.at[kind, offset],
            recv_sem=st_rsem.at[kind, offset],
            device_id={"tp": tp_peer(offset)},
            device_id_type=pl.DeviceIdType.MESH,
        )

    def stat_send(kind):
        for offset in range(1, 8):
            stat_copy(kind, offset).start()

    def stat_total(kind):
        total = stat[kind, 0]
        for offset in range(1, 8):
            stat_copy(kind, offset).wait_recv()
            total = total + stat[kind, offset]
        return total

    def token_sums(square):
        return jnp.sum(jnp.transpose(square), axis=0, keepdims=True)

    def spread(row):
        return jnp.transpose(jnp.broadcast_to(row, (SPAN, SPAN)))

    def head(number):
        return slice(number * DH, (number + 1) * DH)

    stat[0, 0] = jnp.zeros((8, 2 * SPAN), F32)
    for half in (LOW, HIGH):
        square = jnp.zeros((SPAN, DH), F32)
        for h in range(GROUP):
            part = q_ref[offs[half], :, head(h)].astype(F32)
            square = square + part * part
        stat[0, 0, 0:1, half * SPAN:(half + 1) * SPAN] = token_sums(square)
        part = k_ref[offs[half]].astype(F32)
        stat[0, 0, 1:2, half * SPAN:(half + 1) * SPAN] = token_sums(part * part)
    stat_send(0)

    cos_t, sin_t = tab_ref[0], tab_ref[1]
    for half in (LOW, HIGH):
        cos_s = span_ref[0, spans[half]]
        sin_s = span_ref[1, spans[half]]
        rope[half, 0] = cos_s * cos_t - sin_s * sin_t
        rope[half, 1] = sin_s * cos_t + cos_s * sin_t
    for half in (LOW, HIGH):
        for h in range(GROUP):
            part = do_ref[offs[half], :, head(h)]
            dos[half, head(h), :] = part
            dot_[half, :, head(h)] = jnp.transpose(part)

    def rotated(half, part, sign):
        turned = pltpu.roll(part, DH // 2, 1) * rope[half, 1]
        straight = part * rope[half, 0]
        return straight + turned if sign > 0 else straight - turned

    total = stat_total(0)
    q_inv = lax.rsqrt(total[0:1, :] / D + EPS)
    k_inv = lax.rsqrt(total[1:2, :] / KVD + EPS)
    for half in (LOW, HIGH):
        ki[half] = spread(k_inv[:, half * SPAN:(half + 1) * SPAN])
        part = k_ref[offs[half]].astype(F32)
        part = part * ki[half] * kg_ref[...]
        kv[KEY, half, 0] = rotated(half, part, 1).astype(BF16)
        gather_forward(KEY, half, 0)

    hop(VAL, (1, 2, 3, 4))

    for half in (LOW, HIGH):
        qi[half] = spread(q_inv[:, half * SPAN:(half + 1) * SPAN])
        for h in range(GROUP):
            part = q_ref[offs[half], :, head(h)].astype(F32)
            part = part * qi[half] * qg_ref[:, head(h)]
            turned = rotated(half, part, 1).astype(BF16)
            qs[half, head(h), :] = turned
            qt[half, :, head(h)] = jnp.transpose(turned)

    hop(VAL, (5, 6, 7, 8, 9, 10))

    def mm(a, b):
        return jnp.dot(a, b, preferred_element_type=F32)

    def pick(is_low, which, slot):
        return jnp.where(is_low, kv[which, LOW, slot], kv[which, HIGH, slot])

    def values_pass(slot):
        is_low = sel_ref[slot] == 1
        other = 1 - sel_ref[slot]
        v_low, v_other = kv[VAL, LOW, slot], pick(is_low, VAL, slot)
        for start, width in CHUNKS:
            cols = pl.ds(start, width)
            dp_a[slot, :, cols] = mm(v_low, dot_[HIGH, :, cols])
            dp_b[slot, :, cols] = mm(v_other, dot_[other, :, cols])

    def scores(keys, half, cols, d_probs, exps, slot, mask=None):
        s = mm(keys, qt[half, :, cols])
        if mask is not None:
            s = jnp.where(mask, s, NEG)
        top = jnp.max(s, axis=0, keepdims=True)
        e = jnp.exp2(s * C2 - top * C2)
        exps[slot, :, cols] = e
        return (
            top,
            jnp.sum(e, axis=0, keepdims=True),
            jnp.sum(e * d_probs[slot, :, cols], axis=0, keepdims=True),
        )

    def put(tabs, row, cols, stats):
        for tab, value in zip(tabs, stats):
            tab[row, :, cols] = value

    tabs_high, tabs_low = (mh, lh, dh), (ml, ll, dl)

    def keys_pass(slot):
        chosen = sel_ref[slot]
        is_low = chosen == 1
        k_low, k_other = kv[KEY, LOW, slot], pick(is_low, KEY, slot)
        for start, width in CHUNKS:
            cols = pl.ds(start, width)
            put(tabs_high, slot, cols, scores(k_low, HIGH, cols, dp_a, e_a, slot))
            top, total, dots = scores(k_other, 1 - chosen, cols, dp_b, e_b, slot)
            put(tabs_high, slot + 15, cols, (jnp.where(is_low, NEG, top), total, dots))
            put(tabs_low, slot, cols, (jnp.where(is_low, top, NEG), total, dots))

    def own_values():
        for start, width in CHUNKS:
            cols = pl.ds(start, width)
            dp_a[0, :, cols] = mm(kv[VAL, LOW, 0], dot_[HIGH, :, cols])
            dp_b[0, :, cols] = mm(kv[VAL, LOW, 0], dot_[LOW, :, cols])
            dp_b[16, :, cols] = mm(kv[VAL, HIGH, 0], dot_[HIGH, :, cols])

    def own_keys():
        for start, width in CHUNKS:
            cols = pl.ds(start, width)
            shape = (SPAN, width)
            mask = lax.broadcasted_iota(jnp.int32, shape, 0) <= (
                lax.broadcasted_iota(jnp.int32, shape, 1) % SPAN
            )
            put(tabs_high, 0, cols, scores(kv[KEY, LOW, 0], HIGH, cols, dp_a, e_a, 0))
            put(tabs_low, 0, cols, scores(kv[KEY, LOW, 0], LOW, cols, dp_b, e_b, 0, mask))
            put(tabs_high, 31, cols, scores(kv[KEY, HIGH, 0], HIGH, cols, dp_b, e_b, 16, mask))

    own_values()
    lax.fori_loop(1, 9, lambda slot, _: (values_pass(slot), 0)[1], 0)
    hop(KEY, (1, 2, 3, 4))
    own_keys()
    hop(VAL, (11, 12, 13, 14, 15))
    hop(KEY, (5, 6, 7, 8, 9, 10))
    lax.fori_loop(9, 16, lambda slot, _: (values_pass(slot), 0)[1], 0)
    lax.fori_loop(1, 11, lambda slot, _: (keys_pass(slot), 0)[1], 0)
    hop(KEY, (11, 12, 13, 14, 15))
    lax.fori_loop(11, 16, lambda slot, _: (keys_pass(slot), 0)[1], 0)

    def finish(tabs, factors, half):
        tops, sums, dots = (tab[...] for tab in tabs)
        weights = jnp.exp2((tops - jnp.max(tops, axis=0, keepdims=True)) * C2)
        scale = 1.0 / jnp.sum(weights * sums, axis=0, keepdims=True)
        delta[half] = (jnp.sum(weights * dots, axis=0, keepdims=True) * scale)[0]
        factors[...] = weights * scale

    finish(tabs_high, fh, HIGH)
    finish(tabs_low, fl, LOW)

    def grads(exps, d_probs, slot, factor, shift, where):
        for start, width in CHUNKS:
            cols = pl.ds(start, width)
            probs = exps[slot, :, cols] * factor(cols)
            d_scores = probs * (d_probs[slot, :, cols] - shift(cols))
            pb[where, :, cols] = probs.astype(BF16)
            dsb[pl.ds(where * SPAN, SPAN), cols] = d_scores.astype(BF16)

    def rows(where):
        return pl.ds(where * SPAN, SPAN)

    def second_pass(slot):
        chosen = sel_ref[slot]
        is_low = chosen == 1
        other = 1 - chosen
        grads(e_a, dp_a, slot, lambda c: fh[slot, :, c], lambda c: delta[HIGH, :, c], 0)
        grads(
            e_b, dp_b, slot,
            lambda c: fl[slot, :, c] + fh[slot + 15, :, c],
            lambda c: delta[other, :, c], 1,
        )
        for kind, left in ((0, None), (1, None)):
            a_rows = pb[0] if kind == 0 else dsb[rows(0), :]
            b_rows = pb[1] if kind == 0 else dsb[rows(1), :]
            source = dos if kind == 0 else qs
            from_a = mm(a_rows, source[HIGH])
            from_b = mm(b_rows, source[other])
            cb[slot, LOW, kind] = from_a + jnp.where(is_low, from_b, 0.0)
            cb[slot, HIGH, kind] = jnp.where(is_low, 0.0, from_b)
        turned_low = jnp.transpose(kv[KEY, LOW, slot])
        turned_other = jnp.transpose(pick(is_low, KEY, slot))
        none = jnp.zeros_like(turned_other)
        both = jnp.concatenate([turned_low, jnp.where(is_low, none, turned_other)], axis=1)
        only_low = jnp.where(is_low, turned_other, none)
        for start, width in CHUNKS:
            cols = pl.ds(start, width)
            acc[HIGH, :, cols] += mm(both, dsb[0:2 * SPAN, cols])
            acc[LOW, :, cols] += mm(only_low, dsb[rows(1), cols])

    def own_second():
        grads(e_a, dp_a, 0, lambda c: fh[0, :, c], lambda c: delta[HIGH, :, c], 0)
        grads(e_b, dp_b, 16, lambda c: fh[31, :, c], lambda c: delta[HIGH, :, c], 1)
        grads(e_b, dp_b, 0, lambda c: fl[0, :, c], lambda c: delta[LOW, :, c], 2)
        for kind in (0, 1):
            source = dos if kind == 0 else qs
            parts = [pb[i] if kind == 0 else dsb[rows(i), :] for i in range(3)]
            cb[0, LOW, kind] = mm(parts[0], source[HIGH]) + mm(parts[2], source[LOW])
            cb[0, HIGH, kind] = mm(parts[1], source[HIGH])
        turned_low = jnp.transpose(kv[KEY, LOW, 0])
        turned_high = jnp.transpose(kv[KEY, HIGH, 0])
        both = jnp.concatenate([turned_low, turned_high], axis=1)
        for start, width in CHUNKS:
            cols = pl.ds(start, width)
            acc[HIGH, :, cols] += mm(both, dsb[0:2 * SPAN, cols])
            acc[LOW, :, cols] += mm(turned_low, dsb[rows(2), cols])

    acc[...] = jnp.zeros_like(acc)

    FAR, PLUS, MINUS = 0, 1, 2

    def ring_copy(half, first, what):
        step = 3 if what == MINUS else 1
        return pltpu.make_async_remote_copy(
            src_ref=stage.at[half, first, what],
            dst_ref=gotr.at[half, first, what],
            send_sem=rs_ssem.at[half, first, what],
            recv_sem=rs_rsem.at[half, first, what],
            device_id={"ctx": neighbour(half, 1, step)},
            device_id_type=pl.DeviceIdType.MESH,
        )

    def last_copy(half, what):
        step = 3 if what == MINUS else 1
        return pltpu.make_async_remote_copy(
            src_ref=pstage.at[half, what],
            dst_ref=gotp.at[half, what],
            send_sem=ps_ssem.at[half, what],
            recv_sem=ps_rsem.at[half, what],
            device_id={"ctx": neighbour(half, 0, step)},
            device_id_type=pl.DeviceIdType.MESH,
        )

    def send_far(half, first):
        stage[half, first, FAR] = cb[slot_of(half, first, 2), half].astype(BF16)
        ring_copy(half, first, FAR).start()

    def send_minus(half, first):
        stage[half, first, MINUS] = cb[slot_of(half, first, 3), half].astype(BF16)
        ring_copy(half, first, MINUS).start()

    def send_plus(half, first):
        ring_copy(half, first, FAR).wait_recv()
        mixed = cb[slot_of(half, first, 1), half] + gotr[half, first, FAR].astype(F32)
        stage[half, first, PLUS] = mixed.astype(BF16)
        ring_copy(half, first, PLUS).start()

    def ring_sum(half, first):
        ring_copy(half, first, PLUS).wait_recv()
        ring_copy(half, first, MINUS).wait_recv()
        return (
            cb[slot_of(half, first, 0), half]
            + gotr[half, first, PLUS].astype(F32)
            + gotr[half, first, MINUS].astype(F32)
        )

    def last_send(half, what):
        first = {FAR: 2, PLUS: 1, MINUS: 3}[what]
        total = ring_sum(half, first)
        if what == PLUS:
            last_copy(half, FAR).wait_recv()
            total = total + gotp[half, FAR].astype(F32)
        pstage[half, what] = total.astype(BF16)
        last_copy(half, what).start()

    def last_sum(half):
        total = ring_sum(half, 0)
        last_copy(half, PLUS).wait_recv()
        last_copy(half, MINUS).wait_recv()
        return total + gotp[half, PLUS].astype(F32) + gotp[half, MINUS].astype(F32)

    events = {slot: [] for slot in range(SLOTS)}
    for slot in range(1, SLOTS):
        for half in (LOW, HIGH):
            first, second = primary_view(half, slot)
            if second == 2:
                events[slot].append((send_far, half, first))
            if second == 3:
                events[slot].append((send_minus, half, first))
            if second == 1:
                events[max(slot - 2, 1)].append((send_plus, half, first))
    for half in (LOW, HIGH):
        events[4].append((last_send, half, FAR))

    def run_events(slot):
        for action, half, argument in events[slot]:
            action(half, argument)

    def second_step(number, carry):
        slot = SLOTS - 1 - number
        second_pass(slot)
        for which in range(1, SLOTS):
            if events[which]:
                pl.when(slot == which)(functools.partial(run_events, which))
        return carry

    lax.fori_loop(0, SLOTS - 1, second_step, 0)
    own_second()
    for what in (PLUS, MINUS):
        for half in (LOW, HIGH):
            last_send(half, what)

    stat[1, 0] = jnp.zeros((8, 2 * SPAN), F32)
    gain_buf[0] = jnp.zeros((8, DH), F32)
    for half in (LOW, HIGH):
        inner = jnp.zeros((SPAN, DH), F32)
        for h in range(GROUP):
            d_rot = jnp.transpose(acc[half, :, head(h)]) * SCALE
            d_norm = rotated(half, d_rot, -1)
            q_hat = q_ref[offs[half], :, head(h)].astype(F32) * qi[half]
            gain_buf[0, h:h + 1, :] += jnp.sum(d_norm * q_hat, axis=0, keepdims=True)
            scaled = d_norm * qg_ref[:, head(h)]
            sg[half, :, head(h)] = scaled
            inner = inner + scaled * q_hat
        stat[1, 0, 0:1, half * SPAN:(half + 1) * SPAN] = token_sums(inner)
    stat_send(1)

    stat[2, 0] = jnp.zeros((8, 2 * SPAN), F32)
    for half in (LOW, HIGH):
        summed = last_sum(half)
        dkn[1, half] = summed[0]
        d_norm = rotated(half, summed[1] * SCALE, -1)
        k_hat = k_ref[offs[half]].astype(F32) * ki[half]
        gain_buf[0, 5:6, :] += jnp.sum(d_norm * k_hat, axis=0, keepdims=True)
        scaled = d_norm * kg_ref[...]
        dkn[0, half] = scaled
        stat[2, 0, 0:1, half * SPAN:(half + 1) * SPAN] = token_sums(scaled * k_hat)
    stat_send(2)

    def gain_copy(slot):
        return pltpu.make_async_remote_copy(
            src_ref=gain_buf.at[0],
            dst_ref=gain_buf.at[slot],
            send_sem=gn_ssem.at[slot],
            recv_sem=gn_rsem.at[slot],
            device_id={"ctx": at_offset(*ORDER[slot])},
            device_id_type=pl.DeviceIdType.MESH,
        )

    for slot in range(1, SLOTS):
        gain_copy(slot).start()

    q_inner = stat_total(1)[0:1, :] / D
    for half in (LOW, HIGH):
        inner = spread(q_inner[:, half * SPAN:(half + 1) * SPAN])
        for h in range(GROUP):
            q_hat = q_ref[offs[half], :, head(h)].astype(F32) * qi[half]
            sg[half, :, head(h)] = qi[half] * (sg[half, :, head(h)] - q_hat * inner)

    first_half = jnp.where(s0 < s1, LOW, HIGH)
    for place, half in ((0, first_half), (1, 1 - first_half)):
        dq_out[place * SPAN:(place + 1) * SPAN, :] = sg[half].astype(BF16)
        dv_out[place * SPAN:(place + 1) * SPAN, :] = dkn[1, half].astype(BF16)

    k_inner = stat_total(2)[0:1, :] / KVD
    for half in (LOW, HIGH):
        inner = spread(k_inner[:, half * SPAN:(half + 1) * SPAN])
        k_hat = k_ref[offs[half]].astype(F32) * ki[half]
        dkn[0, half] = ki[half] * (dkn[0, half] - k_hat * inner)
    for place, half in ((0, first_half), (1, 1 - first_half)):
        dk_out[place * SPAN:(place + 1) * SPAN, :] = dkn[0, half].astype(BF16)

    total = gain_buf[0]
    for slot in range(1, SLOTS):
        gain_copy(slot).wait_recv()
        total = total + gain_buf[slot]
    for h in range(GROUP):
        dqg_out[:, head(h)] = total[h:h + 1, :]
    dkg_out[...] = total[5:6, :]

    for which in (KEY, VAL):
        for half in (LOW, HIGH):
            for slot in range(SLOTS):
                for axis, step, dst in gather_sends(half, slot):
                    gather_copy(which, half, slot, axis, step, dst).wait_send()
    for half in (LOW, HIGH):
        for what in (FAR, PLUS, MINUS):
            for first in range(RING):
                ring_copy(half, first, what).wait_send()
            last_copy(half, what).wait_send()
    for kind in range(3):
        for offset in range(1, 8):
            stat_copy(kind, offset).wait_send()
    for slot in range(1, SLOTS):
        gain_copy(slot).wait_send()


def per_device(q_raw, k_raw, values, d_out, q_gain, k_gain, span_order):
    token_table, span_table = tables()
    vmem = pl.BlockSpec(memory_space=pltpu.VMEM)
    smem = pl.BlockSpec(memory_space=pltpu.SMEM)
    tile = (SPAN, DH)
    dma = pltpu.SemaphoreType.DMA
    wide = (SPAN, QW)
    scratch = [
        pltpu.SMEM((SLOTS,), jnp.int32),
        pltpu.VMEM((2, 2, SLOTS) + tile, BF16),
        pltpu.VMEM((2, QW, DH), BF16),
        pltpu.VMEM((2, DH, QW), BF16),
        pltpu.VMEM((2, QW, DH), BF16),
        pltpu.VMEM((2, DH, QW), BF16),
        pltpu.VMEM((2, 2) + tile, F32),
        pltpu.VMEM((2,) + tile, F32),
        pltpu.VMEM((2,) + tile, F32),
        pltpu.VMEM((16,) + wide, F32),
        pltpu.VMEM((17,) + wide, F32),
        pltpu.VMEM((16,) + wide, F32),
        pltpu.VMEM((17,) + wide, F32),
        pltpu.VMEM((32, 1, QW), F32),
        pltpu.VMEM((32, 1, QW), F32),
        pltpu.VMEM((32, 1, QW), F32),
        pltpu.VMEM((16, 1, QW), F32),
        pltpu.VMEM((16, 1, QW), F32),
        pltpu.VMEM((16, 1, QW), F32),
        pltpu.VMEM((32, 1, QW), F32),
        pltpu.VMEM((16, 1, QW), F32),
        pltpu.VMEM((2, 1, QW), F32),
        pltpu.VMEM((3,) + wide, BF16),
        pltpu.VMEM((3 * SPAN, QW), BF16),
        pltpu.VMEM((2,) + wide, F32),
        pltpu.VMEM((SLOTS, 2, 2) + tile, F32),
        pltpu.VMEM((2, RING, 3, 2) + tile, BF16),
        pltpu.VMEM((2, RING, 3, 2) + tile, BF16),
        pltpu.VMEM((2, 3, 2) + tile, BF16),
        pltpu.VMEM((2, 3, 2) + tile, BF16),
        pltpu.VMEM((2,) + wide, F32),
        pltpu.VMEM((2, 2) + tile, F32),
        pltpu.VMEM((3, 8, 8, 2 * SPAN), F32),
        pltpu.VMEM((SLOTS, 8, DH), F32),
        dma((2, 2, SLOTS)), dma((2, 2, SLOTS)),
        dma((2, RING, 3)), dma((2, RING, 3)),
        dma((2, 3)), dma((2, 3)),
        dma((3, 8)), dma((3, 8)),
        dma((SLOTS,)), dma((SLOTS,)),
    ]
    rows = 2 * SPAN
    outs = pl.pallas_call(
        kernel,
        out_shape=(
            jax.ShapeDtypeStruct((rows, QW), BF16),
            jax.ShapeDtypeStruct((rows, DH), BF16),
            jax.ShapeDtypeStruct((rows, DH), BF16),
            jax.ShapeDtypeStruct((1, QW), F32),
            jax.ShapeDtypeStruct((1, DH), F32),
        ),
        in_specs=[smem] + [vmem] * 8,
        out_specs=(vmem,) * 5,
        scratch_shapes=scratch,
        compiler_params=pltpu.CompilerParams(
            collective_id=0, has_side_effects=True, vmem_limit_bytes=56 * 2**20
        ),
    )(
        span_order,
        q_raw.reshape(2, SPAN, QW), k_raw.reshape(2, SPAN, DH),
        values.reshape(2, SPAN, DH), d_out.reshape(2, SPAN, QW),
        q_gain.reshape(1, QW), k_gain.reshape(1, DH), token_table, span_table,
    )
    return outs[0], outs[1], outs[2], outs[3].reshape(QW), outs[4].reshape(DH)


def solution(mesh):
    return jax.shard_map(
        per_device,
        mesh=mesh,
        in_specs=(
            P("ctx", "tp"),
            P("ctx", "tp"),
            P("ctx", "tp"),
            P("ctx", "tp"),
            P("tp"),
            P("tp"),
            P(),
        ),
        out_specs=(P("ctx", "tp"), P("ctx", "tp"), P("ctx", "tp"), P("tp"), P("tp")),
        check_vma=False,
    )
```

```python
import functools
import math

import jax
import jax.numpy as jnp
import numpy as np
from jax import lax
from jax.experimental import pallas as pl
from jax.experimental.pallas import tpu as pltpu
from jax.sharding import PartitionSpec as P

D = 5120
KVD = 1024
DH = 128
SPAN = 128
SPANS = 32
GROUP = 5
QW = GROUP * DH
EPS = 1e-06
THETA = 500000.0
NEG = -1e30
SCALE = DH ** (-0.5)
C2 = SCALE * math.log2(math.e)
RING = 4
SLOTS = 16
F32 = jnp.float32
BF16 = jnp.bfloat16

ORDER = [
    (0, 0), (0, 3), (3, 0), (0, 1), (1, 0), (0, 2), (2, 0), (3, 3),
    (1, 3), (3, 1), (1, 1), (3, 2), (2, 3), (1, 2), (2, 1), (2, 2),
]
SLOT = {pair: number for number, pair in enumerate(ORDER)}
MIRROR = [SLOT[(-oz % RING, -ox % RING)] for oz, ox in ORDER]
RINGS = [(0, 1), (0, 2), (0, 3), (1, 0), (2, 0), (3, 0)]
CHUNKS = ((0, 256), (256, 256), (512, 128))
LOW, HIGH = 0, 1
KEY, VAL = 0, 1


def primary_view(half, slot):
    oz, ox = ORDER[slot]
    return (ox, oz) if half == LOW else (oz, ox)


def slot_of(half, first, second):
    return SLOT[(second, first)] if half == LOW else SLOT[(first, second)]


def gather_sends(half, slot):
    first, second = primary_view(half, slot)
    sends = []
    if second == 0:
        if first == 0:
            sends += [(0, step, slot_of(half, -step % RING, 0)) for step in (1, 3, 2)]
        sends += [(1, step, slot_of(half, first, -step % RING)) for step in (1, 3)]
        if first == 2:
            sends += [(1, 2, slot_of(half, first, 2))]
    if second == 3 and first != 2:
        sends += [(1, 1, slot_of(half, first, 2))]
    return sends


def tables():
    freq = np.asarray(
        np.float32(THETA) ** (-np.arange(DH // 2, dtype=np.float32) / np.float32(DH // 2)),
        np.float64,
    )
    sign = np.concatenate([-np.ones(DH // 2), np.ones(DH // 2)])

    def pair(numbers):
        angle = np.asarray(numbers, np.float64)[:, None] * freq[None, :]
        cos = np.concatenate([np.cos(angle)] * 2, axis=1)
        sin = np.concatenate([np.sin(angle)] * 2, axis=1) * sign
        return cos, sin

    cos_t, sin_t = pair(np.arange(SPAN))
    cos_s, sin_s = pair(np.arange(SPANS) * SPAN)
    token = np.stack([cos_t, sin_t]).astype(np.float32)
    span = np.stack([cos_s, sin_s])[:, :, None, :].astype(np.float32)
    return jnp.asarray(token), jnp.asarray(span)


def kernel(
    so_ref, q_in, k_in, v_in, do_in, qg_in, kg_in, tab_in, span_in,
    dq_hbm, dk_hbm, dv_hbm, dqg_hbm, dkg_hbm,
    qg_ref, kg_ref, tab_ref, span_ref, dq_out, dk_out, dv_out, dqg_out, dkg_out,
    sel_ref, low_ref, q_ref, k_ref, v_ref, do_ref,
    kv, kr, qs, qt, dos, dot_, rope, qi, ki,
    e_a, e_b, dp_a, dp_b, mh, lh, dh, ml, ll, dl, fh, fl, delta,
    pb, dsb, acc, cb, stage, gotr, pstage, gotp, sg, dkn,
    stat, inv_buf, gain_buf,
    in_sem, out_sem, relay, ag_ssem, ag_rsem, rs_ssem, rs_rsem, ps_ssem, ps_rsem,
    st_ssem, st_rsem, iv_ssem, iv_rsem, gn_ssem, gn_rsem,
):
    loads = [
        pltpu.make_async_copy(source, target, in_sem.at[number])
        for number, (source, target) in enumerate(
            (
                (k_in, k_ref), (v_in, v_ref), (q_in, q_ref), (do_in, do_ref),
                (qg_in, qg_ref), (kg_in, kg_ref), (tab_in, tab_ref), (span_in, span_ref),
            )
        )
    ]
    for load in loads:
        load.start()

    ctx = lax.axis_index("ctx")
    tp = lax.axis_index("tp")
    z, x = ctx // RING, ctx % RING
    flip = tp % 2
    turned_z = [z] + [(z + jnp.where(flip == 0, o, RING - o)) % RING for o in (1, 2, 3)]
    turned_x = [x] + [(x + jnp.where(flip == 0, o, RING - o)) % RING for o in (1, 2, 3)]
    peers = {(oz, ox): turned_z[oz] * RING + turned_x[ox] for oz, ox in ORDER}
    tp_peers = [(tp + offset) % 8 for offset in range(8)]

    def to_ctx(pair):
        return {"ctx": peers[pair]}

    barrier = pltpu.get_barrier_semaphore()
    for pair in RINGS:
        pl.semaphore_signal(
            barrier, inc=1, device_id=to_ctx(pair), device_id_type=pl.DeviceIdType.MESH
        )
    for offset in range(1, 8):
        pl.semaphore_signal(
            barrier, inc=1, device_id={"tp": tp_peers[offset]},
            device_id_type=pl.DeviceIdType.MESH,
        )

    s0, s1 = so_ref[2 * ctx], so_ref[2 * ctx + 1]
    low = jnp.minimum(s0, s1)
    offs = (jnp.where(s0 < s1, 0, 1), jnp.where(s0 < s1, 1, 0))
    low_ref[0] = low
    for slot in range(1, SLOTS):
        other = peers[ORDER[slot]]
        a = jnp.minimum(so_ref[2 * other], so_ref[2 * other + 1])
        low_ref[slot] = a
        sel_ref[slot] = jnp.where(a < low, 1, 0)

    loads[0].wait()
    loads[1].wait()
    for half in (LOW, HIGH):
        kv[half, 0, KEY] = k_ref[offs[half]]
        kv[half, 0, VAL] = v_ref[offs[half]]

    pl.semaphore_wait(barrier, 13)

    axis_of = {LOW: ("x", "z"), HIGH: ("z", "x")}

    def neighbour(half, axis, step):
        return to_ctx((step, 0) if axis_of[half][axis] == "z" else (0, step))

    def gather_copy(half, slot, axis, step, dst):
        return pltpu.make_async_remote_copy(
            src_ref=kv.at[half, slot],
            dst_ref=kv.at[half, dst],
            send_sem=ag_ssem.at[half, dst],
            recv_sem=ag_rsem.at[half, dst],
            device_id=neighbour(half, axis, step),
            device_id_type=pl.DeviceIdType.MESH,
        )

    def gather_forward(half, slot):
        for axis, step, dst in gather_sends(half, slot):
            gather_copy(half, slot, axis, step, dst).start()

    def hop(slots):
        for slot in slots:
            for half in (LOW, HIGH):
                gather_copy(half, slot, 0, 1, slot).wait_recv()
                gather_forward(half, slot)

    gather_forward(LOW, 0)
    gather_forward(HIGH, 0)
    for pair in RINGS[3:]:
        pl.semaphore_signal(
            relay, inc=1, device_id=to_ctx(pair), device_id_type=pl.DeviceIdType.MESH
        )

    def stat_copy(kind, offset):
        return pltpu.make_async_remote_copy(
            src_ref=stat.at[kind, 0],
            dst_ref=stat.at[kind, offset],
            send_sem=st_ssem.at[kind, offset],
            recv_sem=st_rsem.at[kind, offset],
            device_id={"tp": tp_peers[offset]},
            device_id_type=pl.DeviceIdType.MESH,
        )

    def stat_send(kind):
        for offset in range(1, 8):
            stat_copy(kind, offset).start()

    def stat_total(kind):
        total = stat[kind, 0]
        for offset in range(1, 8):
            stat_copy(kind, offset).wait_recv()
            total = total + stat[kind, offset]
        return total

    def token_sums(square):
        return jnp.sum(jnp.transpose(square), axis=0, keepdims=True)

    def spread(row):
        return jnp.transpose(jnp.broadcast_to(row, (SPAN, SPAN)))

    def head(number):
        return slice(number * DH, (number + 1) * DH)

    def q_gain_row(h):
        return qg_ref[head(h)].reshape(1, DH)

    def k_gain_row():
        return kg_ref[...].reshape(1, DH)

    for load in loads[2:]:
        load.wait()
    stat[0, 0] = jnp.zeros((8, SPAN), F32)
    for half in (LOW, HIGH):
        square = jnp.zeros((SPAN, DH), F32)
        for h in range(GROUP):
            part = q_ref[offs[half], :, head(h)].astype(F32)
            square = square + part * part
        stat[0, 0, half:half + 1, :] = token_sums(square)
        part = kv[half, 0, KEY].astype(F32)
        stat[0, 0, 2 + half:3 + half, :] = token_sums(part * part)
    stat_send(0)

    def rope_tables(span):
        cos_t, sin_t = tab_ref[0], tab_ref[1]
        cos_s, sin_s = span_ref[0, span], span_ref[1, span]
        return cos_s * cos_t - sin_s * sin_t, sin_s * cos_t + cos_s * sin_t

    for half, span in ((LOW, low), (HIGH, SPANS - 1 - low)):
        rope[half, 0], rope[half, 1] = rope_tables(span)
    for half in (LOW, HIGH):
        for h in range(GROUP):
            part = do_ref[offs[half], :, head(h)]
            dos[half, head(h), :] = part
            dot_[half, :, head(h)] = jnp.transpose(part)

    def rotated(half, part, sign):
        turned = pltpu.roll(part, DH // 2, 1) * rope[half, 1]
        straight = part * rope[half, 0]
        return straight + turned if sign > 0 else straight - turned

    total = stat_total(0)
    pl.semaphore_wait(relay, 3)
    inv_buf[0] = lax.rsqrt(total / KVD + EPS)
    q_inv = lax.rsqrt(total / D + EPS)

    def inv_copy(slot):
        return pltpu.make_async_remote_copy(
            src_ref=inv_buf.at[0],
            dst_ref=inv_buf.at[MIRROR[slot]],
            send_sem=iv_ssem.at[slot],
            recv_sem=iv_rsem.at[MIRROR[slot]],
            device_id=to_ctx(ORDER[slot]),
            device_id_type=pl.DeviceIdType.MESH,
        )

    for slot in range(1, SLOTS):
        inv_copy(slot).start()

    hop((1, 2, 3, 4))

    for half in (LOW, HIGH):
        ki[half] = spread(inv_buf[0, 2 + half:3 + half, :])
        part = kv[half, 0, KEY].astype(F32) * ki[half] * k_gain_row()
        kr[half, 0] = rotated(half, part, 1).astype(BF16)
        qi[half] = spread(q_inv[half:half + 1, :])
        for h in range(GROUP):
            part = q_ref[offs[half], :, head(h)].astype(F32) * qi[half] * q_gain_row(h)
            turned = rotated(half, part, 1).astype(BF16)
            qs[half, head(h), :] = turned
            qt[half, :, head(h)] = jnp.transpose(turned)

    hop((5, 6))

    def mm(a, b):
        return jnp.dot(a, b, preferred_element_type=F32)

    def pick(is_low, low_rows, high_rows):
        return jnp.where(is_low, low_rows, high_rows)

    def key_rows(half, slot):
        span = low_ref[slot] if half == LOW else SPANS - 1 - low_ref[slot]
        cos, sin = rope_tables(span)
        part = kv[half, slot, KEY].astype(F32)
        part = part * spread(inv_buf[slot, 2 + half:3 + half, :]) * k_gain_row()
        part = part * cos + pltpu.roll(part, DH // 2, 1) * sin
        kr[half, slot] = part.astype(BF16)

    def values_pass(slot):
        is_low = sel_ref[slot] == 1
        other = 1 - sel_ref[slot]
        v_low = kv[LOW, slot, VAL]
        v_other = pick(is_low, v_low, kv[HIGH, slot, VAL])
        for start, width in CHUNKS:
            cols = pl.ds(start, width)
            dp_a[slot, :, cols] = mm(v_low, dot_[HIGH, :, cols])
            dp_b[slot, :, cols] = mm(v_other, dot_[other, :, cols])

    def scores(keys, half, cols, d_probs, exps, slot, mask=None):
        s = mm(keys, qt[half, :, cols])
        if mask is not None:
            s = jnp.where(mask, s, NEG)
        top = jnp.max(s, axis=0, keepdims=True)
        e = jnp.exp2(s * C2 - top * C2)
        exps[slot, :, cols] = e
        return (
            top,
            jnp.sum(e, axis=0, keepdims=True),
            jnp.sum(e * d_probs[slot, :, cols], axis=0, keepdims=True),
        )

    def put(tabs, row, cols, stats):
        for tab, value in zip(tabs, stats):
            tab[row, :, cols] = value

    tabs_high, tabs_low = (mh, lh, dh), (ml, ll, dl)

    def keys_pass(slot):
        chosen = sel_ref[slot]
        is_low = chosen == 1
        for half in (LOW, HIGH):
            key_rows(half, slot)
        k_low = kr[LOW, slot]
        k_other = pick(is_low, k_low, kr[HIGH, slot])
        for start, width in CHUNKS:
            cols = pl.ds(start, width)
            put(tabs_high, slot, cols, scores(k_low, HIGH, cols, dp_a, e_a, slot))
            top, total, dots = scores(k_other, 1 - chosen, cols, dp_b, e_b, slot)
            put(tabs_high, slot + 15, cols, (jnp.where(is_low, NEG, top), total, dots))
            put(tabs_low, slot, cols, (jnp.where(is_low, top, NEG), total, dots))

    def own_values():
        for start, width in CHUNKS:
            cols = pl.ds(start, width)
            dp_a[0, :, cols] = mm(kv[LOW, 0, VAL], dot_[HIGH, :, cols])
            dp_b[0, :, cols] = mm(kv[LOW, 0, VAL], dot_[LOW, :, cols])
            dp_b[16, :, cols] = mm(kv[HIGH, 0, VAL], dot_[HIGH, :, cols])

    def own_keys():
        for start, width in CHUNKS:
            cols = pl.ds(start, width)
            shape = (SPAN, width)
            mask = lax.broadcasted_iota(jnp.int32, shape, 0) <= (
                lax.broadcasted_iota(jnp.int32, shape, 1) % SPAN
            )
            put(tabs_high, 0, cols, scores(kr[LOW, 0], HIGH, cols, dp_a, e_a, 0))
            put(tabs_low, 0, cols, scores(kr[LOW, 0], LOW, cols, dp_b, e_b, 0, mask))
            put(tabs_high, 31, cols, scores(kr[HIGH, 0], HIGH, cols, dp_b, e_b, 16, mask))

    def over(first, last, step):
        lax.fori_loop(first, last, lambda slot, _: (step(slot), 0)[1], 0)

    own_values()
    own_keys()
    over(1, 5, values_pass)
    hop((7, 8, 9))
    over(5, 7, values_pass)
    for slot in range(1, SLOTS):
        inv_copy(MIRROR[slot]).wait_recv()
    over(1, 7, keys_pass)
    hop((10, 11, 12))
    over(7, 13, values_pass)
    over(7, 10, keys_pass)
    hop((13, 14, 15))
    over(10, 13, keys_pass)
    over(13, 16, values_pass)
    over(13, 16, keys_pass)

    def finish(tabs, factors, half):
        tops, sums, dots = (tab[...] for tab in tabs)
        weights = jnp.exp2((tops - jnp.max(tops, axis=0, keepdims=True)) * C2)
        scale = 1.0 / jnp.sum(weights * sums, axis=0, keepdims=True)
        delta[half] = (jnp.sum(weights * dots, axis=0, keepdims=True) * scale)[0]
        factors[...] = weights * scale

    finish(tabs_high, fh, HIGH)
    finish(tabs_low, fl, LOW)

    def grads(exps, d_probs, slot, factor, shift, where):
        for start, width in CHUNKS:
            cols = pl.ds(start, width)
            probs = exps[slot, :, cols] * factor(cols)
            d_scores = probs * (d_probs[slot, :, cols] - shift(cols))
            pb[where, :, cols] = probs.astype(BF16)
            dsb[pl.ds(where * SPAN, SPAN), cols] = d_scores.astype(BF16)

    def rows(where):
        return pl.ds(where * SPAN, SPAN)

    def second_pass(slot):
        chosen = sel_ref[slot]
        is_low = chosen == 1
        other = 1 - chosen
        grads(e_a, dp_a, slot, lambda c: fh[slot, :, c], lambda c: delta[HIGH, :, c], 0)
        grads(
            e_b, dp_b, slot,
            lambda c: fl[slot, :, c] + fh[slot + 15, :, c],
            lambda c: delta[other, :, c], 1,
        )
        for kind, left in ((0, None), (1, None)):
            a_rows = pb[0] if kind == 0 else dsb[rows(0), :]
            b_rows = pb[1] if kind == 0 else dsb[rows(1), :]
            source = dos if kind == 0 else qs
            from_a = mm(a_rows, source[HIGH])
            from_b = mm(b_rows, source[other])
            cb[slot, LOW, kind] = from_a + jnp.where(is_low, from_b, 0.0)
            cb[slot, HIGH, kind] = jnp.where(is_low, 0.0, from_b)
        turned_low = jnp.transpose(kr[LOW, slot])
        turned_other = jnp.transpose(pick(is_low, kr[LOW, slot], kr[HIGH, slot]))
        none = jnp.zeros_like(turned_other)
        both = jnp.concatenate([turned_low, jnp.where(is_low, none, turned_other)], axis=1)
        only_low = jnp.where(is_low, turned_other, none)
        for start, width in CHUNKS:
            cols = pl.ds(start, width)
            acc[HIGH, :, cols] += mm(both, dsb[0:2 * SPAN, cols])
            acc[LOW, :, cols] += mm(only_low, dsb[rows(1), cols])

    def own_second():
        grads(e_a, dp_a, 0, lambda c: fh[0, :, c], lambda c: delta[HIGH, :, c], 0)
        grads(e_b, dp_b, 16, lambda c: fh[31, :, c], lambda c: delta[HIGH, :, c], 1)
        grads(e_b, dp_b, 0, lambda c: fl[0, :, c], lambda c: delta[LOW, :, c], 2)
        for kind in (0, 1):
            source = dos if kind == 0 else qs
            parts = [pb[i] if kind == 0 else dsb[rows(i), :] for i in range(3)]
            cb[0, LOW, kind] = mm(parts[0], source[HIGH]) + mm(parts[2], source[LOW])
            cb[0, HIGH, kind] = mm(parts[1], source[HIGH])
        turned_low = jnp.transpose(kr[LOW, 0])
        turned_high = jnp.transpose(kr[HIGH, 0])
        both = jnp.concatenate([turned_low, turned_high], axis=1)
        for start, width in CHUNKS:
            cols = pl.ds(start, width)
            acc[HIGH, :, cols] += mm(both, dsb[0:2 * SPAN, cols])
            acc[LOW, :, cols] += mm(turned_low, dsb[rows(2), cols])

    acc[...] = jnp.zeros_like(acc)

    def ring_copy(half, first, second):
        return pltpu.make_async_remote_copy(
            src_ref=stage.at[half, first, second],
            dst_ref=gotr.at[half, first, second],
            send_sem=rs_ssem.at[half, first, second],
            recv_sem=rs_rsem.at[half, first, second],
            device_id=neighbour(half, 1, second),
            device_id_type=pl.DeviceIdType.MESH,
        )

    def last_copy(half, first):
        return pltpu.make_async_remote_copy(
            src_ref=pstage.at[half, first],
            dst_ref=gotp.at[half, first],
            send_sem=ps_ssem.at[half, first],
            recv_sem=ps_rsem.at[half, first],
            device_id=neighbour(half, 0, first),
            device_id_type=pl.DeviceIdType.MESH,
        )

    def ring_send(half, slot):
        first, second = primary_view(half, slot)
        if second:
            stage[half, first, second] = cb[slot, half].astype(BF16)
            ring_copy(half, first, second).start()

    def ring_sum(half, first):
        total = cb[slot_of(half, first, 0), half]
        for second in (1, 2, 3):
            ring_copy(half, first, second).wait_recv()
            total = total + gotr[half, first, second].astype(F32)
        return total

    def last_send(first):
        for half in (LOW, HIGH):
            pstage[half, first] = ring_sum(half, first).astype(BF16)
            last_copy(half, first).start()

    def last_sum(half):
        total = ring_sum(half, 0)
        for first in (2, 1, 3):
            last_copy(half, first).wait_recv()
            total = total + gotp[half, first].astype(F32)
        return total

    def run_events(slot):
        for half in (LOW, HIGH):
            ring_send(half, slot)
        if slot == 2:
            last_send(2)

    def second_step(number, carry):
        slot = SLOTS - 1 - number
        second_pass(slot)
        for which in range(1, SLOTS):
            pl.when(slot == which)(functools.partial(run_events, which))
        return carry

    lax.fori_loop(0, SLOTS - 1, second_step, 0)
    own_second()
    stat[1, 0] = jnp.zeros((8, SPAN), F32)
    gain_buf[0] = jnp.zeros((8, DH), F32)
    for half in (LOW, HIGH):
        inner = jnp.zeros((SPAN, DH), F32)
        for h in range(GROUP):
            d_rot = jnp.transpose(acc[half, :, head(h)]) * SCALE
            d_norm = rotated(half, d_rot, -1)
            q_hat = q_ref[offs[half], :, head(h)].astype(F32) * qi[half]
            gain_buf[0, h:h + 1, :] += jnp.sum(d_norm * q_hat, axis=0, keepdims=True)
            scaled = d_norm * q_gain_row(h)
            sg[half, :, head(h)] = scaled
            inner = inner + scaled * q_hat
        stat[1, 0, half:half + 1, :] = token_sums(inner)
    stat_send(1)

    last_send(1)
    last_send(3)

    q_inner = stat_total(1) / D
    for half in (LOW, HIGH):
        inner = spread(q_inner[half:half + 1, :])
        for h in range(GROUP):
            q_hat = q_ref[offs[half], :, head(h)].astype(F32) * qi[half]
            sg[half, :, head(h)] = qi[half] * (sg[half, :, head(h)] - q_hat * inner)

    first_half = jnp.where(s0 < s1, LOW, HIGH)
    places = ((0, first_half), (1, 1 - first_half))
    for place, half in places:
        dq_out[place * SPAN:(place + 1) * SPAN, :] = sg[half].astype(BF16)

    def store(number, source, target):
        return pltpu.make_async_copy(source, target, out_sem.at[number])

    stores = [
        store(number, source, target)
        for number, (source, target) in enumerate(
            (
                (dq_out, dq_hbm), (dk_out, dk_hbm), (dv_out, dv_hbm),
                (dqg_out, dqg_hbm), (dkg_out, dkg_hbm),
            )
        )
    ]
    stores[0].start()

    stat[2, 0] = jnp.zeros((8, SPAN), F32)
    for half in (LOW, HIGH):
        summed = last_sum(half)
        dkn[1, half] = summed[0]
        d_norm = rotated(half, summed[1] * SCALE, -1)
        k_hat = kv[half, 0, KEY].astype(F32) * ki[half]
        gain_buf[0, 5:6, :] += jnp.sum(d_norm * k_hat, axis=0, keepdims=True)
        scaled = d_norm * k_gain_row()
        dkn[0, half] = scaled
        stat[2, 0, half:half + 1, :] = token_sums(scaled * k_hat)

    def gain_copy(slot):
        return pltpu.make_async_remote_copy(
            src_ref=gain_buf.at[0],
            dst_ref=gain_buf.at[slot],
            send_sem=gn_ssem.at[slot],
            recv_sem=gn_rsem.at[slot],
            device_id=to_ctx(ORDER[slot]),
            device_id_type=pl.DeviceIdType.MESH,
        )

    for slot in range(SLOTS - 1, 0, -1):
        gain_copy(slot).start()
    stat_send(2)

    for place, half in places:
        dv_out[place * SPAN:(place + 1) * SPAN, :] = dkn[1, half].astype(BF16)
    stores[2].start()

    k_inner = stat_total(2) / KVD
    for half in (LOW, HIGH):
        inner = spread(k_inner[half:half + 1, :])
        k_hat = kv[half, 0, KEY].astype(F32) * ki[half]
        dkn[0, half] = ki[half] * (dkn[0, half] - k_hat * inner)
    for place, half in places:
        dk_out[place * SPAN:(place + 1) * SPAN, :] = dkn[0, half].astype(BF16)
    stores[1].start()

    total = gain_buf[0]
    for slot in range(1, SLOTS):
        gain_copy(slot).wait_recv()
        total = total + gain_buf[slot]
    for h in range(GROUP):
        dqg_out[head(h)] = total[h:h + 1, :].reshape(DH)
    dkg_out[...] = total[5:6, :].reshape(DH)
    stores[3].start()
    stores[4].start()

    for item in stores:
        item.wait()
    for half in (LOW, HIGH):
        for slot in range(SLOTS):
            for axis, step, dst in gather_sends(half, slot):
                gather_copy(half, slot, axis, step, dst).wait_send()
            first, second = primary_view(half, slot)
            if second:
                ring_copy(half, first, second).wait_send()
        for first in (1, 2, 3):
            last_copy(half, first).wait_send()
    for kind in range(3):
        for offset in range(1, 8):
            stat_copy(kind, offset).wait_send()
    for slot in range(1, SLOTS):
        inv_copy(slot).wait_send()
        gain_copy(slot).wait_send()


def pass_on(*refs):
    for source, target in zip(refs[:5], refs[5:]):
        target[...] = source[...]


def per_device(q_raw, k_raw, values, d_out, q_gain, k_gain, span_order):
    token_table, span_table = tables()
    smem = pl.BlockSpec(memory_space=pltpu.SMEM)
    tile = (SPAN, DH)
    dma = pltpu.SemaphoreType.DMA
    wide = (SPAN, QW)
    scratch = [
        pltpu.VMEM((QW,), F32), pltpu.VMEM((DH,), F32),
        pltpu.VMEM((2,) + tile, F32), pltpu.VMEM((2, SPANS, 1, DH), F32),
        pltpu.VMEM((2 * SPAN, QW), BF16), pltpu.VMEM((2 * SPAN, DH), BF16),
        pltpu.VMEM((2 * SPAN, DH), BF16), pltpu.VMEM((QW,), F32), pltpu.VMEM((DH,), F32),
        pltpu.SMEM((SLOTS,), jnp.int32),
        pltpu.SMEM((SLOTS,), jnp.int32),
        pltpu.VMEM((2,) + wide, BF16),
        pltpu.VMEM((2,) + tile, BF16),
        pltpu.VMEM((2,) + tile, BF16),
        pltpu.VMEM((2,) + wide, BF16),
        pltpu.VMEM((2, SLOTS, 2) + tile, BF16),
        pltpu.VMEM((2, SLOTS) + tile, BF16),
        pltpu.VMEM((2, QW, DH), BF16),
        pltpu.VMEM((2, DH, QW), BF16),
        pltpu.VMEM((2, QW, DH), BF16),
        pltpu.VMEM((2, DH, QW), BF16),
        pltpu.VMEM((2, 2) + tile, F32),
        pltpu.VMEM((2,) + tile, F32),
        pltpu.VMEM((2,) + tile, F32),
        pltpu.VMEM((16,) + wide, F32),
        pltpu.VMEM((17,) + wide, F32),
        pltpu.VMEM((16,) + wide, F32),
        pltpu.VMEM((17,) + wide, F32),
        pltpu.VMEM((32, 1, QW), F32),
        pltpu.VMEM((32, 1, QW), F32),
        pltpu.VMEM((32, 1, QW), F32),
        pltpu.VMEM((16, 1, QW), F32),
        pltpu.VMEM((16, 1, QW), F32),
        pltpu.VMEM((16, 1, QW), F32),
        pltpu.VMEM((32, 1, QW), F32),
        pltpu.VMEM((16, 1, QW), F32),
        pltpu.VMEM((2, 1, QW), F32),
        pltpu.VMEM((3,) + wide, BF16),
        pltpu.VMEM((3 * SPAN, QW), BF16),
        pltpu.VMEM((2,) + wide, F32),
        pltpu.VMEM((SLOTS, 2, 2) + tile, F32),
        pltpu.VMEM((2, RING, RING, 2) + tile, BF16),
        pltpu.VMEM((2, RING, RING, 2) + tile, BF16),
        pltpu.VMEM((2, RING, 2) + tile, BF16),
        pltpu.VMEM((2, RING, 2) + tile, BF16),
        pltpu.VMEM((2,) + wide, F32),
        pltpu.VMEM((2, 2) + tile, F32),
        pltpu.VMEM((3, 8, 8, SPAN), F32),
        pltpu.VMEM((SLOTS, 8, SPAN), F32),
        pltpu.VMEM((SLOTS, 8, DH), F32),
        dma((8,)), dma((5,)), pltpu.SemaphoreType.REGULAR,
        dma((2, SLOTS)), dma((2, SLOTS)),
        dma((2, RING, RING)), dma((2, RING, RING)),
        dma((2, RING)), dma((2, RING)),
        dma((3, 8)), dma((3, 8)),
        dma((SLOTS,)), dma((SLOTS,)),
        dma((SLOTS,)), dma((SLOTS,)),
    ]
    rows = 2 * SPAN
    shapes = (
        jax.ShapeDtypeStruct((rows, QW), BF16),
        jax.ShapeDtypeStruct((rows, DH), BF16),
        jax.ShapeDtypeStruct((rows, DH), BF16),
        jax.ShapeDtypeStruct((QW,), F32),
        jax.ShapeDtypeStruct((DH,), F32),
    )
    vmem = pl.BlockSpec(memory_space=pltpu.VMEM)
    hbm = pl.BlockSpec(memory_space=pltpu.HBM)
    results = pl.pallas_call(
        kernel,
        out_shape=shapes,
        in_specs=[smem] + [hbm] * 8,
        out_specs=(hbm,) * 5,
        scratch_shapes=scratch,
        compiler_params=pltpu.CompilerParams(
            collective_id=0, has_side_effects=True, vmem_limit_bytes=60 * 2**20
        ),
    )(
        span_order,
        q_raw.reshape(2, SPAN, QW), k_raw.reshape(2, SPAN, DH),
        values.reshape(2, SPAN, DH), d_out.reshape(2, SPAN, QW),
        q_gain, k_gain, token_table, span_table,
    )
    return pl.pallas_call(
        pass_on, out_shape=shapes, in_specs=[vmem] * 5, out_specs=(vmem,) * 5,
        compiler_params=pltpu.CompilerParams(vmem_limit_bytes=60 * 2**20),
    )(*results)


def solution(mesh):
    return jax.shard_map(
        per_device,
        mesh=mesh,
        in_specs=(
            P("ctx", "tp"),
            P("ctx", "tp"),
            P("ctx", "tp"),
            P("ctx", "tp"),
            P("tp"),
            P("tp"),
            P(),
        ),
        out_specs=(P("ctx", "tp"), P("ctx", "tp"), P("ctx", "tp"), P("tp"), P("tp")),
        check_vma=False,
    )
```

```python
import math

import jax
import jax.numpy as jnp
import numpy as np
from jax import lax
from jax.experimental import pallas as pl
from jax.experimental.pallas import tpu as pltpu
from jax.sharding import PartitionSpec as P

D = 5120
KVD = 1024
DH = 128
SPAN = 128
SPANS = 32
GROUP = 5
QW = GROUP * DH
EPS = 1e-06
THETA = 500000.0
NEG = -1e30
SCALE = DH ** (-0.5)
C2 = SCALE * math.log2(math.e)
RING = 4
SLOTS = 16
F32 = jnp.float32
BF16 = jnp.bfloat16

ORDER = [
    (0, 0), (0, 3), (3, 0), (0, 1), (1, 0), (0, 2), (2, 0), (3, 3),
    (1, 3), (3, 1), (1, 1), (3, 2), (2, 3), (1, 2), (2, 1), (2, 2),
]
SLOT = {pair: number for number, pair in enumerate(ORDER)}
MIRROR = [SLOT[(-oz % RING, -ox % RING)] for oz, ox in ORDER]
RINGS = [(0, 1), (0, 2), (0, 3), (1, 0), (2, 0), (3, 0)]
CHUNKS = ((0, 256), (256, 256), (512, 128))
LOW, HIGH = 0, 1
KEY, VAL = 0, 1


def primary_view(half, slot):
    oz, ox = ORDER[slot]
    return (ox, oz) if half == LOW else (oz, ox)


def slot_of(half, first, second):
    return SLOT[(second, first)] if half == LOW else SLOT[(first, second)]


def gather_sends(half, slot):
    first, second = primary_view(half, slot)
    sends = []
    if second == 0:
        if first == 0:
            sends += [(0, step, slot_of(half, -step % RING, 0)) for step in (1, 3, 2)]
        sends += [(1, step, slot_of(half, first, -step % RING)) for step in (1, 3)]
        if first == 2:
            sends += [(1, 2, slot_of(half, first, 2))]
    if second == 3 and first != 2:
        sends += [(1, 1, slot_of(half, first, 2))]
    return sends


def tables():
    freq = np.asarray(
        np.float32(THETA) ** (-np.arange(DH // 2, dtype=np.float32) / np.float32(DH // 2)),
        np.float64,
    )
    sign = np.concatenate([-np.ones(DH // 2), np.ones(DH // 2)])

    def pair(numbers):
        angle = np.asarray(numbers, np.float64)[:, None] * freq[None, :]
        cos = np.concatenate([np.cos(angle)] * 2, axis=1)
        sin = np.concatenate([np.sin(angle)] * 2, axis=1) * sign
        return cos, sin

    cos_t, sin_t = pair(np.arange(SPAN))
    cos_s, sin_s = pair(np.arange(SPANS) * SPAN)
    token = np.stack([cos_t, sin_t]).astype(np.float32)
    span = np.stack([cos_s, sin_s])[:, :, None, :].astype(np.float32)
    return jnp.asarray(token), jnp.asarray(span)


def kernel(
    so_ref, q_in, k_in, v_in, do_in, qg_in, kg_in, tab_in, span_in,
    dq_hbm, dk_hbm, dv_hbm, dqg_hbm, dkg_hbm,
    qg_ref, kg_ref, tab_ref, span_ref, dq_out, dk_out, dv_out, dqg_out, dkg_out,
    sel_ref, low_ref, q_ref, k_ref, v_ref, do_ref,
    kv, kr, qs, qt, dos, dot_, rope, qi, ki,
    e_a, e_b, dp_a, dp_b, mh, lh, dh, ml, ll, dl, fh, fl, delta,
    pb, dsb, acc, cb, stage, gotr, pstage, gotp, sg, dkn,
    stat, inv_buf, gain_buf,
    in_sem, out_sem, relay, ag_ssem, ag_rsem, rs_ssem, rs_rsem, ps_ssem, ps_rsem,
    st_ssem, st_rsem, iv_ssem, iv_rsem, gn_ssem, gn_rsem,
):
    loads = [
        pltpu.make_async_copy(source, target, in_sem.at[number])
        for number, (source, target) in enumerate(
            (
                (k_in, k_ref), (v_in, v_ref), (q_in, q_ref), (do_in, do_ref),
                (qg_in, qg_ref), (kg_in, kg_ref), (tab_in, tab_ref), (span_in, span_ref),
            )
        )
    ]
    for load in loads:
        load.start()

    ctx = lax.axis_index("ctx")
    tp = lax.axis_index("tp")
    z, x = ctx // RING, ctx % RING
    flip = tp % 2
    turned_z = [z] + [(z + jnp.where(flip == 0, o, RING - o)) % RING for o in (1, 2, 3)]
    turned_x = [x] + [(x + jnp.where(flip == 0, o, RING - o)) % RING for o in (1, 2, 3)]
    peers = {(oz, ox): turned_z[oz] * RING + turned_x[ox] for oz, ox in ORDER}
    tp_peers = [(tp + offset) % 8 for offset in range(8)]

    def to_ctx(pair):
        return {"ctx": peers[pair]}

    barrier = pltpu.get_barrier_semaphore()
    for pair in RINGS:
        pl.semaphore_signal(
            barrier, inc=1, device_id=to_ctx(pair), device_id_type=pl.DeviceIdType.MESH
        )
    for offset in range(1, 8):
        pl.semaphore_signal(
            barrier, inc=1, device_id={"tp": tp_peers[offset]},
            device_id_type=pl.DeviceIdType.MESH,
        )

    s0, s1 = so_ref[2 * ctx], so_ref[2 * ctx + 1]
    low = jnp.minimum(s0, s1)
    offs = (jnp.where(s0 < s1, 0, 1), jnp.where(s0 < s1, 1, 0))
    low_ref[0] = low
    for slot in range(1, SLOTS):
        other = peers[ORDER[slot]]
        a = jnp.minimum(so_ref[2 * other], so_ref[2 * other + 1])
        low_ref[slot] = a
        sel_ref[slot] = jnp.where(a < low, 1, 0)

    loads[0].wait()
    loads[1].wait()
    for half in (LOW, HIGH):
        kv[half, 0, KEY] = k_ref[offs[half]]
        kv[half, 0, VAL] = v_ref[offs[half]]

    pl.semaphore_wait(barrier, 13)

    axis_of = {LOW: ("x", "z"), HIGH: ("z", "x")}

    def neighbour(half, axis, step):
        return to_ctx((step, 0) if axis_of[half][axis] == "z" else (0, step))

    def gather_copy(half, slot, axis, step, dst):
        return pltpu.make_async_remote_copy(
            src_ref=kv.at[half, slot],
            dst_ref=kv.at[half, dst],
            send_sem=ag_ssem.at[half, dst],
            recv_sem=ag_rsem.at[half, dst],
            device_id=neighbour(half, axis, step),
            device_id_type=pl.DeviceIdType.MESH,
        )

    def gather_forward(half, slot):
        for axis, step, dst in gather_sends(half, slot):
            gather_copy(half, slot, axis, step, dst).start()

    def hop(slots):
        for slot in slots:
            for half in (LOW, HIGH):
                gather_copy(half, slot, 0, 1, slot).wait_recv()
                gather_forward(half, slot)

    gather_forward(LOW, 0)
    gather_forward(HIGH, 0)
    for pair in RINGS[3:]:
        pl.semaphore_signal(
            relay, inc=1, device_id=to_ctx(pair), device_id_type=pl.DeviceIdType.MESH
        )

    def stat_copy(kind, offset):
        return pltpu.make_async_remote_copy(
            src_ref=stat.at[kind, 0],
            dst_ref=stat.at[kind, offset],
            send_sem=st_ssem.at[kind, offset],
            recv_sem=st_rsem.at[kind, offset],
            device_id={"tp": tp_peers[offset]},
            device_id_type=pl.DeviceIdType.MESH,
        )

    def stat_send(kind):
        for offset in range(1, 8):
            stat_copy(kind, offset).start()

    def stat_total(kind):
        total = stat[kind, 0]
        for offset in range(1, 8):
            stat_copy(kind, offset).wait_recv()
            total = total + stat[kind, offset]
        return total

    def token_sums(square):
        return jnp.sum(jnp.transpose(square), axis=0, keepdims=True)

    def spread(row):
        return jnp.transpose(jnp.broadcast_to(row, (SPAN, SPAN)))

    def head(number):
        return slice(number * DH, (number + 1) * DH)

    def q_gain_row(h):
        return qg_ref[head(h)].reshape(1, DH)

    def k_gain_row():
        return kg_ref[...].reshape(1, DH)

    for load in loads[2:]:
        load.wait()
    stat[0, 0] = jnp.zeros((8, SPAN), F32)
    for half in (LOW, HIGH):
        square = jnp.zeros((SPAN, DH), F32)
        for h in range(GROUP):
            part = q_ref[offs[half], :, head(h)].astype(F32)
            square = square + part * part
        stat[0, 0, half:half + 1, :] = token_sums(square)
        part = kv[half, 0, KEY].astype(F32)
        stat[0, 0, 2 + half:3 + half, :] = token_sums(part * part)
    stat_send(0)

    def rope_tables(span):
        cos_t, sin_t = tab_ref[0], tab_ref[1]
        cos_s, sin_s = span_ref[0, span], span_ref[1, span]
        return cos_s * cos_t - sin_s * sin_t, sin_s * cos_t + cos_s * sin_t

    for half, span in ((LOW, low), (HIGH, SPANS - 1 - low)):
        rope[half, 0], rope[half, 1] = rope_tables(span)
    for half in (LOW, HIGH):
        for h in range(GROUP):
            part = do_ref[offs[half], :, head(h)]
            dos[half, head(h), :] = part
            dot_[half, :, head(h)] = jnp.transpose(part)

    def rotated(half, part, sign):
        turned = pltpu.roll(part, DH // 2, 1) * rope[half, 1]
        straight = part * rope[half, 0]
        return straight + turned if sign > 0 else straight - turned

    total = stat_total(0)
    pl.semaphore_wait(relay, 3)
    inv_buf[0] = lax.rsqrt(total / KVD + EPS)
    q_inv = lax.rsqrt(total / D + EPS)

    def inv_copy(slot):
        return pltpu.make_async_remote_copy(
            src_ref=inv_buf.at[0],
            dst_ref=inv_buf.at[MIRROR[slot]],
            send_sem=iv_ssem.at[slot],
            recv_sem=iv_rsem.at[MIRROR[slot]],
            device_id=to_ctx(ORDER[slot]),
            device_id_type=pl.DeviceIdType.MESH,
        )

    for slot in range(1, SLOTS):
        inv_copy(slot).start()

    hop((1, 2, 3, 4))

    for half in (LOW, HIGH):
        ki[half] = spread(inv_buf[0, 2 + half:3 + half, :])
        part = kv[half, 0, KEY].astype(F32) * ki[half] * k_gain_row()
        kr[half, 0] = rotated(half, part, 1).astype(BF16)
        qi[half] = spread(q_inv[half:half + 1, :])
        for h in range(GROUP):
            part = q_ref[offs[half], :, head(h)].astype(F32) * qi[half] * q_gain_row(h)
            turned = rotated(half, part, 1).astype(BF16)
            qs[half, head(h), :] = turned
            qt[half, :, head(h)] = jnp.transpose(turned)

    hop((5, 6))

    def mm(a, b):
        return jnp.dot(a, b, preferred_element_type=F32)

    def pick(is_low, low_rows, high_rows):
        return jnp.where(is_low, low_rows, high_rows)

    def key_rows(half, slot):
        span = low_ref[slot] if half == LOW else SPANS - 1 - low_ref[slot]
        cos, sin = rope_tables(span)
        part = kv[half, slot, KEY].astype(F32)
        part = part * spread(inv_buf[slot, 2 + half:3 + half, :]) * k_gain_row()
        part = part * cos + pltpu.roll(part, DH // 2, 1) * sin
        kr[half, slot] = part.astype(BF16)

    def values_pass(slot):
        is_low = sel_ref[slot] == 1
        other = 1 - sel_ref[slot]
        v_low = kv[LOW, slot, VAL]
        v_other = pick(is_low, v_low, kv[HIGH, slot, VAL])
        for start, width in CHUNKS:
            cols = pl.ds(start, width)
            dp_a[slot, :, cols] = mm(v_low, dot_[HIGH, :, cols])
            dp_b[slot, :, cols] = mm(v_other, dot_[other, :, cols])

    def scores(keys, half, cols, d_probs, exps, slot, mask=None):
        s = mm(keys, qt[half, :, cols])
        if mask is not None:
            s = jnp.where(mask, s, NEG)
        top = jnp.max(s, axis=0, keepdims=True)
        e = jnp.exp2(s * C2 - top * C2)
        exps[slot, :, cols] = e
        return (
            top,
            jnp.sum(e, axis=0, keepdims=True),
            jnp.sum(e * d_probs[slot, :, cols], axis=0, keepdims=True),
        )

    def put(tabs, row, cols, stats):
        for tab, value in zip(tabs, stats):
            tab[row, :, cols] = value

    tabs_high, tabs_low = (mh, lh, dh), (ml, ll, dl)

    def keys_pass(slot):
        chosen = sel_ref[slot]
        is_low = chosen == 1
        for half in (LOW, HIGH):
            key_rows(half, slot)
        k_low = kr[LOW, slot]
        k_other = pick(is_low, k_low, kr[HIGH, slot])
        for start, width in CHUNKS:
            cols = pl.ds(start, width)
            put(tabs_high, slot, cols, scores(k_low, HIGH, cols, dp_a, e_a, slot))
            top, total, dots = scores(k_other, 1 - chosen, cols, dp_b, e_b, slot)
            put(tabs_high, slot + 15, cols, (jnp.where(is_low, NEG, top), total, dots))
            put(tabs_low, slot, cols, (jnp.where(is_low, top, NEG), total, dots))

    def own_values():
        for start, width in CHUNKS:
            cols = pl.ds(start, width)
            dp_a[0, :, cols] = mm(kv[LOW, 0, VAL], dot_[HIGH, :, cols])
            dp_b[0, :, cols] = mm(kv[LOW, 0, VAL], dot_[LOW, :, cols])
            dp_b[16, :, cols] = mm(kv[HIGH, 0, VAL], dot_[HIGH, :, cols])

    def own_keys():
        for start, width in CHUNKS:
            cols = pl.ds(start, width)
            shape = (SPAN, width)
            mask = lax.broadcasted_iota(jnp.int32, shape, 0) <= (
                lax.broadcasted_iota(jnp.int32, shape, 1) % SPAN
            )
            put(tabs_high, 0, cols, scores(kr[LOW, 0], HIGH, cols, dp_a, e_a, 0))
            put(tabs_low, 0, cols, scores(kr[LOW, 0], LOW, cols, dp_b, e_b, 0, mask))
            put(tabs_high, 31, cols, scores(kr[HIGH, 0], HIGH, cols, dp_b, e_b, 16, mask))

    def over(first, last, step):
        for slot in range(first, last):
            step(slot)

    own_values()
    own_keys()
    over(1, 5, values_pass)
    hop((7, 8, 9))
    over(5, 7, values_pass)
    for slot in range(1, SLOTS):
        inv_copy(MIRROR[slot]).wait_recv()
    over(1, 7, keys_pass)
    hop((10, 11, 12))
    over(7, 13, values_pass)
    over(7, 10, keys_pass)
    hop((13, 14, 15))
    over(10, 13, keys_pass)
    over(13, 16, values_pass)
    over(13, 16, keys_pass)

    def finish(tabs, factors, half):
        tops, sums, dots = (tab[...] for tab in tabs)
        weights = jnp.exp2((tops - jnp.max(tops, axis=0, keepdims=True)) * C2)
        scale = 1.0 / jnp.sum(weights * sums, axis=0, keepdims=True)
        delta[half] = (jnp.sum(weights * dots, axis=0, keepdims=True) * scale)[0]
        factors[...] = weights * scale

    finish(tabs_high, fh, HIGH)
    finish(tabs_low, fl, LOW)

    def grads(exps, d_probs, slot, factor, shift, where):
        for start, width in CHUNKS:
            cols = pl.ds(start, width)
            probs = exps[slot, :, cols] * factor(cols)
            d_scores = probs * (d_probs[slot, :, cols] - shift(cols))
            pb[where, :, cols] = probs.astype(BF16)
            dsb[pl.ds(where * SPAN, SPAN), cols] = d_scores.astype(BF16)

    def rows(where):
        return pl.ds(where * SPAN, SPAN)

    def second_pass(slot):
        chosen = sel_ref[slot]
        is_low = chosen == 1
        other = 1 - chosen
        grads(e_a, dp_a, slot, lambda c: fh[slot, :, c], lambda c: delta[HIGH, :, c], 0)
        grads(
            e_b, dp_b, slot,
            lambda c: fl[slot, :, c] + fh[slot + 15, :, c],
            lambda c: delta[other, :, c], 1,
        )
        for kind, left in ((0, None), (1, None)):
            a_rows = pb[0] if kind == 0 else dsb[rows(0), :]
            b_rows = pb[1] if kind == 0 else dsb[rows(1), :]
            source = dos if kind == 0 else qs
            from_a = mm(a_rows, source[HIGH])
            from_b = mm(b_rows, source[other])
            cb[slot, LOW, kind] = from_a + jnp.where(is_low, from_b, 0.0)
            cb[slot, HIGH, kind] = jnp.where(is_low, 0.0, from_b)
        turned_low = jnp.transpose(kr[LOW, slot])
        turned_other = jnp.transpose(pick(is_low, kr[LOW, slot], kr[HIGH, slot]))
        none = jnp.zeros_like(turned_other)
        both = jnp.concatenate([turned_low, jnp.where(is_low, none, turned_other)], axis=1)
        only_low = jnp.where(is_low, turned_other, none)
        for start, width in CHUNKS:
            cols = pl.ds(start, width)
            acc[HIGH, :, cols] += mm(both, dsb[0:2 * SPAN, cols])
            acc[LOW, :, cols] += mm(only_low, dsb[rows(1), cols])

    def own_second():
        grads(e_a, dp_a, 0, lambda c: fh[0, :, c], lambda c: delta[HIGH, :, c], 0)
        grads(e_b, dp_b, 16, lambda c: fh[31, :, c], lambda c: delta[HIGH, :, c], 1)
        grads(e_b, dp_b, 0, lambda c: fl[0, :, c], lambda c: delta[LOW, :, c], 2)
        for kind in (0, 1):
            source = dos if kind == 0 else qs
            parts = [pb[i] if kind == 0 else dsb[rows(i), :] for i in range(3)]
            cb[0, LOW, kind] = mm(parts[0], source[HIGH]) + mm(parts[2], source[LOW])
            cb[0, HIGH, kind] = mm(parts[1], source[HIGH])
        turned_low = jnp.transpose(kr[LOW, 0])
        turned_high = jnp.transpose(kr[HIGH, 0])
        both = jnp.concatenate([turned_low, turned_high], axis=1)
        for start, width in CHUNKS:
            cols = pl.ds(start, width)
            acc[HIGH, :, cols] += mm(both, dsb[0:2 * SPAN, cols])
            acc[LOW, :, cols] += mm(turned_low, dsb[rows(2), cols])

    acc[...] = jnp.zeros_like(acc)

    def ring_copy(half, first, second):
        return pltpu.make_async_remote_copy(
            src_ref=stage.at[half, first, second],
            dst_ref=gotr.at[half, first, second],
            send_sem=rs_ssem.at[half, first, second],
            recv_sem=rs_rsem.at[half, first, second],
            device_id=neighbour(half, 1, 1 if first and second == 2 else second),
            device_id_type=pl.DeviceIdType.MESH,
        )

    def last_copy(half, first):
        return pltpu.make_async_remote_copy(
            src_ref=pstage.at[half, first],
            dst_ref=gotp.at[half, first],
            send_sem=ps_ssem.at[half, first],
            recv_sem=ps_rsem.at[half, first],
            device_id=neighbour(half, 0, first),
            device_id_type=pl.DeviceIdType.MESH,
        )

    def ring_send(half, slot):
        first, second = primary_view(half, slot)
        if second > 1 or (second == 1 and first == 0):
            stage[half, first, second] = cb[slot, half].astype(BF16)
            ring_copy(half, first, second).start()

    def near_send(first):
        for half in (LOW, HIGH):
            ring_copy(half, first, 2).wait_recv()
            mixed = cb[slot_of(half, first, 1), half] + gotr[half, first, 2].astype(F32)
            stage[half, first, 1] = mixed.astype(BF16)
            ring_copy(half, first, 1).start()

    def ring_sum(half, first):
        total = cb[slot_of(half, first, 0), half]
        for second in (1, 3) if first else (1, 2, 3):
            ring_copy(half, first, second).wait_recv()
            total = total + gotr[half, first, second].astype(F32)
        return total

    def gain_part(half, first, d_rot):
        slot = slot_of(half, first, 0)
        span = low_ref[slot] if half == LOW else SPANS - 1 - low_ref[slot]
        cos, sin = rope_tables(span)
        d_norm = d_rot * cos - pltpu.roll(d_rot, DH // 2, 1) * sin
        k_hat = kv[half, slot, KEY].astype(F32) * spread(inv_buf[slot, 2 + half:3 + half, :])
        gain_buf[0, 5:6, :] += jnp.sum(d_norm * k_hat, axis=0, keepdims=True)

    def last_send(first):
        totals = []
        for half in (LOW, HIGH):
            totals.append(ring_sum(half, first))
            pstage[half, first] = totals[half].astype(BF16)
            last_copy(half, first).start()
        for half in (LOW, HIGH):
            gain_part(half, first, totals[half][1] * SCALE)

    steps = (15, 14, 13, 12, 11, 7, 9, 8, 6, 5, 10, 4, 3, 2, 1)
    near = {10: 2, 4: 1, 2: 3}
    for slot in steps:
        second_pass(slot)
        for half in (LOW, HIGH):
            ring_send(half, slot)
        if slot in near:
            near_send(near[slot])
    own_second()

    stat[1, 0] = jnp.zeros((8, SPAN), F32)
    gain_buf[0] = jnp.zeros((8, DH), F32)
    for half in (LOW, HIGH):
        inner = jnp.zeros((SPAN, DH), F32)
        for h in range(GROUP):
            d_rot = jnp.transpose(acc[half, :, head(h)]) * SCALE
            d_norm = rotated(half, d_rot, -1)
            q_hat = q_ref[offs[half], :, head(h)].astype(F32) * qi[half]
            gain_buf[0, h:h + 1, :] += jnp.sum(d_norm * q_hat, axis=0, keepdims=True)
            scaled = d_norm * q_gain_row(h)
            sg[half, :, head(h)] = scaled
            inner = inner + scaled * q_hat
        stat[1, 0, half:half + 1, :] = token_sums(inner)
    stat_send(1)

    for first in (2, 1, 3):
        last_send(first)

    q_inner = stat_total(1) / D
    for half in (LOW, HIGH):
        inner = spread(q_inner[half:half + 1, :])
        for h in range(GROUP):
            q_hat = q_ref[offs[half], :, head(h)].astype(F32) * qi[half]
            sg[half, :, head(h)] = qi[half] * (sg[half, :, head(h)] - q_hat * inner)

    first_half = jnp.where(s0 < s1, LOW, HIGH)
    places = ((0, first_half), (1, 1 - first_half))
    for place, half in places:
        dq_out[place * SPAN:(place + 1) * SPAN, :] = sg[half].astype(BF16)

    def store(number, source, target):
        return pltpu.make_async_copy(source, target, out_sem.at[number])

    stores = [
        store(number, source, target)
        for number, (source, target) in enumerate(
            (
                (dq_out, dq_hbm), (dk_out, dk_hbm), (dv_out, dv_hbm),
                (dqg_out, dqg_hbm), (dkg_out, dkg_hbm),
            )
        )
    ]
    stores[0].start()

    totals = [ring_sum(half, 0) for half in (LOW, HIGH)]
    for half in (LOW, HIGH):
        gain_part(half, 0, totals[half][1] * SCALE)

    def gain_copy(slot):
        return pltpu.make_async_remote_copy(
            src_ref=gain_buf.at[0],
            dst_ref=gain_buf.at[slot],
            send_sem=gn_ssem.at[slot],
            recv_sem=gn_rsem.at[slot],
            device_id=to_ctx(ORDER[slot]),
            device_id_type=pl.DeviceIdType.MESH,
        )

    for slot in range(SLOTS - 1, 0, -1):
        gain_copy(slot).start()

    stat[2, 0] = jnp.zeros((8, SPAN), F32)
    for half in (LOW, HIGH):
        total = totals[half]
        for first in (2, 1, 3):
            last_copy(half, first).wait_recv()
            total = total + gotp[half, first].astype(F32)
        dkn[1, half] = total[0]
        d_norm = rotated(half, total[1] * SCALE, -1)
        k_hat = kv[half, 0, KEY].astype(F32) * ki[half]
        scaled = d_norm * k_gain_row()
        dkn[0, half] = scaled
        stat[2, 0, half:half + 1, :] = token_sums(scaled * k_hat)
    stat_send(2)

    for place, half in places:
        dv_out[place * SPAN:(place + 1) * SPAN, :] = dkn[1, half].astype(BF16)
    stores[2].start()

    k_inner = stat_total(2) / KVD
    for half in (LOW, HIGH):
        inner = spread(k_inner[half:half + 1, :])
        k_hat = kv[half, 0, KEY].astype(F32) * ki[half]
        dkn[0, half] = ki[half] * (dkn[0, half] - k_hat * inner)
    for place, half in places:
        dk_out[place * SPAN:(place + 1) * SPAN, :] = dkn[0, half].astype(BF16)
    stores[1].start()

    total = gain_buf[0]
    for slot in range(1, SLOTS):
        gain_copy(slot).wait_recv()
        total = total + gain_buf[slot]
    for h in range(GROUP):
        dqg_out[head(h)] = total[h:h + 1, :].reshape(DH)
    dkg_out[...] = total[5:6, :].reshape(DH)
    stores[3].start()
    stores[4].start()

    for item in stores:
        item.wait()
    for half in (LOW, HIGH):
        for slot in range(SLOTS):
            for axis, step, dst in gather_sends(half, slot):
                gather_copy(half, slot, axis, step, dst).wait_send()
            first, second = primary_view(half, slot)
            if second:
                ring_copy(half, first, second).wait_send()
        for first in (1, 2, 3):
            last_copy(half, first).wait_send()
    for kind in range(3):
        for offset in range(1, 8):
            stat_copy(kind, offset).wait_send()
    for slot in range(1, SLOTS):
        inv_copy(slot).wait_send()
        gain_copy(slot).wait_send()


def pass_on(*refs):
    for source, target in zip(refs[:5], refs[5:]):
        target[...] = source[...]


def per_device(q_raw, k_raw, values, d_out, q_gain, k_gain, span_order):
    token_table, span_table = tables()
    smem = pl.BlockSpec(memory_space=pltpu.SMEM)
    tile = (SPAN, DH)
    dma = pltpu.SemaphoreType.DMA
    wide = (SPAN, QW)
    scratch = [
        pltpu.VMEM((QW,), F32), pltpu.VMEM((DH,), F32),
        pltpu.VMEM((2,) + tile, F32), pltpu.VMEM((2, SPANS, 1, DH), F32),
        pltpu.VMEM((2 * SPAN, QW), BF16), pltpu.VMEM((2 * SPAN, DH), BF16),
        pltpu.VMEM((2 * SPAN, DH), BF16), pltpu.VMEM((QW,), F32), pltpu.VMEM((DH,), F32),
        pltpu.SMEM((SLOTS,), jnp.int32),
        pltpu.SMEM((SLOTS,), jnp.int32),
        pltpu.VMEM((2,) + wide, BF16),
        pltpu.VMEM((2,) + tile, BF16),
        pltpu.VMEM((2,) + tile, BF16),
        pltpu.VMEM((2,) + wide, BF16),
        pltpu.VMEM((2, SLOTS, 2) + tile, BF16),
        pltpu.VMEM((2, SLOTS) + tile, BF16),
        pltpu.VMEM((2, QW, DH), BF16),
        pltpu.VMEM((2, DH, QW), BF16),
        pltpu.VMEM((2, QW, DH), BF16),
        pltpu.VMEM((2, DH, QW), BF16),
        pltpu.VMEM((2, 2) + tile, F32),
        pltpu.VMEM((2,) + tile, F32),
        pltpu.VMEM((2,) + tile, F32),
        pltpu.VMEM((16,) + wide, F32),
        pltpu.VMEM((17,) + wide, F32),
        pltpu.VMEM((16,) + wide, F32),
        pltpu.VMEM((17,) + wide, F32),
        pltpu.VMEM((32, 1, QW), F32),
        pltpu.VMEM((32, 1, QW), F32),
        pltpu.VMEM((32, 1, QW), F32),
        pltpu.VMEM((16, 1, QW), F32),
        pltpu.VMEM((16, 1, QW), F32),
        pltpu.VMEM((16, 1, QW), F32),
        pltpu.VMEM((32, 1, QW), F32),
        pltpu.VMEM((16, 1, QW), F32),
        pltpu.VMEM((2, 1, QW), F32),
        pltpu.VMEM((3,) + wide, BF16),
        pltpu.VMEM((3 * SPAN, QW), BF16),
        pltpu.VMEM((2,) + wide, F32),
        pltpu.VMEM((SLOTS, 2, 2) + tile, F32),
        pltpu.VMEM((2, RING, RING, 2) + tile, BF16),
        pltpu.VMEM((2, RING, RING, 2) + tile, BF16),
        pltpu.VMEM((2, RING, 2) + tile, BF16),
        pltpu.VMEM((2, RING, 2) + tile, BF16),
        pltpu.VMEM((2,) + wide, F32),
        pltpu.VMEM((2, 2) + tile, F32),
        pltpu.VMEM((3, 8, 8, SPAN), F32),
        pltpu.VMEM((SLOTS, 8, SPAN), F32),
        pltpu.VMEM((SLOTS, 8, DH), F32),
        dma((8,)), dma((5,)), pltpu.SemaphoreType.REGULAR,
        dma((2, SLOTS)), dma((2, SLOTS)),
        dma((2, RING, RING)), dma((2, RING, RING)),
        dma((2, RING)), dma((2, RING)),
        dma((3, 8)), dma((3, 8)),
        dma((SLOTS,)), dma((SLOTS,)),
        dma((SLOTS,)), dma((SLOTS,)),
    ]
    rows = 2 * SPAN
    shapes = (
        jax.ShapeDtypeStruct((rows, QW), BF16),
        jax.ShapeDtypeStruct((rows, DH), BF16),
        jax.ShapeDtypeStruct((rows, DH), BF16),
        jax.ShapeDtypeStruct((QW,), F32),
        jax.ShapeDtypeStruct((DH,), F32),
    )
    vmem = pl.BlockSpec(memory_space=pltpu.VMEM)
    hbm = pl.BlockSpec(memory_space=pltpu.HBM)
    results = pl.pallas_call(
        kernel,
        out_shape=shapes,
        in_specs=[smem] + [hbm] * 8,
        out_specs=(hbm,) * 5,
        scratch_shapes=scratch,
        compiler_params=pltpu.CompilerParams(
            collective_id=0, has_side_effects=True, vmem_limit_bytes=60 * 2**20
        ),
    )(
        span_order,
        q_raw.reshape(2, SPAN, QW), k_raw.reshape(2, SPAN, DH),
        values.reshape(2, SPAN, DH), d_out.reshape(2, SPAN, QW),
        q_gain, k_gain, token_table, span_table,
    )
    return pl.pallas_call(
        pass_on, out_shape=shapes, in_specs=[vmem] * 5, out_specs=(vmem,) * 5,
        compiler_params=pltpu.CompilerParams(vmem_limit_bytes=60 * 2**20),
    )(*results)


def solution(mesh):
    return jax.shard_map(
        per_device,
        mesh=mesh,
        in_specs=(
            P("ctx", "tp"),
            P("ctx", "tp"),
            P("ctx", "tp"),
            P("ctx", "tp"),
            P("tp"),
            P("tp"),
            P(),
        ),
        out_specs=(P("ctx", "tp"), P("ctx", "tp"), P("ctx", "tp"), P("tp"), P("tp")),
        check_vma=False,
    )
```

```python
import math

import jax
import jax.numpy as jnp
import numpy as np
from jax import lax
from jax.experimental import pallas as pl
from jax.experimental.pallas import tpu as pltpu
from jax.sharding import PartitionSpec as P

D = 5120
KVD = 1024
DH = 128
SPAN = 128
SPANS = 32
GROUP = 5
QW = GROUP * DH
EPS = 1e-06
THETA = 500000.0
NEG = -1e30
SCALE = DH ** (-0.5)
C2 = SCALE * math.log2(math.e)
RING = 4
SLOTS = 16
F32 = jnp.float32
BF16 = jnp.bfloat16

ORDER = [
    (0, 0), (0, 3), (3, 0), (0, 1), (1, 0), (0, 2), (2, 0), (3, 3),
    (1, 3), (3, 1), (1, 1), (3, 2), (2, 3), (1, 2), (2, 1), (2, 2),
]
SLOT = {pair: number for number, pair in enumerate(ORDER)}
MIRROR = [SLOT[(-oz % RING, -ox % RING)] for oz, ox in ORDER]
RINGS = [(0, 1), (0, 2), (0, 3), (1, 0), (2, 0), (3, 0)]
CHUNKS = ((0, 256), (256, 256), (512, 128))
LOW, HIGH = 0, 1
KEY, VAL = 0, 1


def primary_view(half, slot):
    oz, ox = ORDER[slot]
    return (ox, oz) if half == LOW else (oz, ox)


def slot_of(half, first, second):
    return SLOT[(second, first)] if half == LOW else SLOT[(first, second)]


def gather_sends(half, slot):
    first, second = primary_view(half, slot)
    sends = []
    if second == 0:
        if first == 0:
            sends += [(0, step, slot_of(half, -step % RING, 0)) for step in (1, 3, 2)]
        sends += [(1, step, slot_of(half, first, -step % RING)) for step in (1, 3)]
        if first == 2:
            sends += [(1, 2, slot_of(half, first, 2))]
    if second == 3 and first != 2:
        sends += [(1, 1, slot_of(half, first, 2))]
    return sends


def tables():
    freq = np.asarray(
        np.float32(THETA) ** (-np.arange(DH // 2, dtype=np.float32) / np.float32(DH // 2)),
        np.float64,
    )
    sign = np.concatenate([-np.ones(DH // 2), np.ones(DH // 2)])

    def pair(numbers):
        angle = np.asarray(numbers, np.float64)[:, None] * freq[None, :]
        cos = np.concatenate([np.cos(angle)] * 2, axis=1)
        sin = np.concatenate([np.sin(angle)] * 2, axis=1) * sign
        return cos, sin

    cos_t, sin_t = pair(np.arange(SPAN))
    cos_s, sin_s = pair(np.arange(SPANS) * SPAN)
    token = np.stack([cos_t, sin_t]).astype(np.float32)
    span = np.stack([cos_s, sin_s])[:, :, None, :].astype(np.float32)
    return jnp.asarray(token), jnp.asarray(span)


def kernel(
    so_in, q_in, k_in, v_in, do_in, qg_in, kg_in, tab_in, span_in,
    dq_hbm, dk_hbm, dv_hbm, dqg_hbm, dkg_hbm,
    so_ref, qg_ref, kg_ref, tab_ref, span_ref, dq_out, dk_out, dv_out, dqg_out, dkg_out,
    sel_ref, low_ref, q_ref, k_ref, v_ref, do_ref,
    kv, kr, qs, qt, dos, dot_, rope, qi, ki,
    e_a, e_b, dp_a, dp_b, mh, lh, dh, ml, ll, dl, fh, fl, delta,
    pb, dsb, acc, cb, stage, gotr, pstage, gotp, sg, dkn,
    stat, inv_buf, gain_buf,
    in_sem, out_sem, relay, sent, ag_sem, rest_sem, far_sem, rs_sem, ps_sem, st_sem, small_sem,
):
    order_load = pltpu.make_async_copy(so_in, so_ref, in_sem.at[8])
    order_load.start()
    loads = [
        pltpu.make_async_copy(source, target, in_sem.at[number])
        for number, (source, target) in enumerate(
            (
                (k_in, k_ref), (v_in, v_ref), (q_in, q_ref), (do_in, do_ref),
                (qg_in, qg_ref), (kg_in, kg_ref), (tab_in, tab_ref), (span_in, span_ref),
            )
        )
    ]
    for load in loads:
        load.start()

    ctx = lax.axis_index("ctx")
    tp = lax.axis_index("tp")
    z, x = ctx // RING, ctx % RING
    flip = tp % 2
    turned_z = [z] + [(z + jnp.where(flip == 0, o, RING - o)) % RING for o in (1, 2, 3)]
    turned_x = [x] + [(x + jnp.where(flip == 0, o, RING - o)) % RING for o in (1, 2, 3)]
    peers = {(oz, ox): turned_z[oz] * RING + turned_x[ox] for oz, ox in ORDER}
    tp_peers = [(tp + offset) % 8 for offset in range(8)]

    def to_ctx(pair):
        return {"ctx": peers[pair]}

    barrier = pltpu.get_barrier_semaphore()
    for pair in RINGS:
        pl.semaphore_signal(
            barrier, inc=1, device_id=to_ctx(pair), device_id_type=pl.DeviceIdType.MESH
        )
    for offset in range(1, 8):
        pl.semaphore_signal(
            barrier, inc=1, device_id={"tp": tp_peers[offset]},
            device_id_type=pl.DeviceIdType.MESH,
        )

    order_load.wait()
    s0, s1 = so_ref[2 * ctx], so_ref[2 * ctx + 1]
    low = jnp.minimum(s0, s1)
    offs = (jnp.where(s0 < s1, 0, 1), jnp.where(s0 < s1, 1, 0))
    low_ref[0] = low
    for slot in range(1, SLOTS):
        other = peers[ORDER[slot]]
        a = jnp.minimum(so_ref[2 * other], so_ref[2 * other + 1])
        low_ref[slot] = a
        sel_ref[slot] = jnp.where(a < low, 1, 0)

    loads[0].wait()
    loads[1].wait()
    for half in (LOW, HIGH):
        kv[half, 0, KEY] = k_ref[offs[half]]
        kv[half, 0, VAL] = v_ref[offs[half]]

    pl.semaphore_wait(barrier, 13)

    axis_of = {LOW: ("x", "z"), HIGH: ("z", "x")}

    def neighbour(half, axis, step):
        return to_ctx((step, 0) if axis_of[half][axis] == "z" else (0, step))

    def gather_arrival(half, dst):
        if dst < 10:
            return ag_sem.at[half, dst]
        return rest_sem.at[0 if dst < 13 else 1]

    def gather_copy(half, slot, axis, step, dst):
        return pltpu.make_async_remote_copy(
            src_ref=kv.at[half, slot],
            dst_ref=kv.at[half, dst],
            send_sem=sent.at[0],
            recv_sem=gather_arrival(half, dst),
            device_id=neighbour(half, axis, step),
            device_id_type=pl.DeviceIdType.MESH,
        )

    def gather_forward(half, slot):
        for axis, step, dst in gather_sends(half, slot):
            gather_copy(half, slot, axis, step, dst).start()

    def hop(slots):
        for slot in slots:
            for half in (LOW, HIGH):
                gather_copy(half, slot, 0, 1, slot).wait_recv()
                gather_forward(half, slot)

    def finished(block, sem):
        pltpu.make_async_copy(block, block, sem).wait()

    def rest(first):
        finished(kv.at[:, pl.ds(first, 3)], rest_sem.at[0 if first < 13 else 1])

    gather_forward(LOW, 0)
    gather_forward(HIGH, 0)
    for pair in RINGS[3:]:
        pl.semaphore_signal(
            relay, inc=1, device_id=to_ctx(pair), device_id_type=pl.DeviceIdType.MESH
        )

    def stat_copy(kind, offset):
        return pltpu.make_async_remote_copy(
            src_ref=stat.at[kind, 0],
            dst_ref=stat.at[kind, offset],
            send_sem=sent.at[3],
            recv_sem=st_sem.at[kind],
            device_id={"tp": tp_peers[offset]},
            device_id_type=pl.DeviceIdType.MESH,
        )

    def stat_send(kind):
        for offset in range(1, 8):
            stat_copy(kind, offset).start()

    def stat_total(kind):
        finished(stat.at[kind, pl.ds(1, 7)], st_sem.at[kind])
        total = stat[kind, 0]
        for offset in range(1, 8):
            total = total + stat[kind, offset]
        return total

    def token_sums(square):
        return jnp.sum(jnp.transpose(square), axis=0, keepdims=True)

    def spread(row):
        return jnp.transpose(jnp.broadcast_to(row, (SPAN, SPAN)))

    def head(number):
        return slice(number * DH, (number + 1) * DH)

    def q_gain_row(h):
        return qg_ref[head(h)].reshape(1, DH)

    def k_gain_row():
        return kg_ref[...].reshape(1, DH)

    for load in loads[2:]:
        load.wait()
    stat[0, 0] = jnp.zeros((8, SPAN), F32)
    for half in (LOW, HIGH):
        square = jnp.zeros((SPAN, DH), F32)
        for h in range(GROUP):
            part = q_ref[offs[half], :, head(h)].astype(F32)
            square = square + part * part
        stat[0, 0, half:half + 1, :] = token_sums(square)
        part = kv[half, 0, KEY].astype(F32)
        stat[0, 0, 2 + half:3 + half, :] = token_sums(part * part)
    stat_send(0)

    def rope_tables(span):
        cos_t, sin_t = tab_ref[0], tab_ref[1]
        cos_s, sin_s = span_ref[0, span], span_ref[1, span]
        return cos_s * cos_t - sin_s * sin_t, sin_s * cos_t + cos_s * sin_t

    for half, span in ((LOW, low), (HIGH, SPANS - 1 - low)):
        rope[half, 0], rope[half, 1] = rope_tables(span)
    for half in (LOW, HIGH):
        for h in range(GROUP):
            part = do_ref[offs[half], :, head(h)]
            dos[half, head(h), :] = part
            dot_[half, :, head(h)] = jnp.transpose(part)

    def rotated(half, part, sign):
        turned = pltpu.roll(part, DH // 2, 1) * rope[half, 1]
        straight = part * rope[half, 0]
        return straight + turned if sign > 0 else straight - turned

    total = stat_total(0)
    pl.semaphore_wait(relay, 3)
    inv_buf[0] = lax.rsqrt(total / KVD + EPS)
    q_inv = lax.rsqrt(total / D + EPS)

    def inv_copy(slot):
        return pltpu.make_async_remote_copy(
            src_ref=inv_buf.at[0],
            dst_ref=inv_buf.at[MIRROR[slot]],
            send_sem=sent.at[4],
            recv_sem=small_sem.at[0],
            device_id=to_ctx(ORDER[slot]),
            device_id_type=pl.DeviceIdType.MESH,
        )

    for slot in range(1, SLOTS):
        inv_copy(slot).start()

    hop((1, 2, 3, 4))

    for half in (LOW, HIGH):
        ki[half] = spread(inv_buf[0, 2 + half:3 + half, :])
        part = kv[half, 0, KEY].astype(F32) * ki[half] * k_gain_row()
        kr[half, 0] = rotated(half, part, 1).astype(BF16)
        qi[half] = spread(q_inv[half:half + 1, :])
        for h in range(GROUP):
            part = q_ref[offs[half], :, head(h)].astype(F32) * qi[half] * q_gain_row(h)
            turned = rotated(half, part, 1).astype(BF16)
            qs[half, head(h), :] = turned
            qt[half, :, head(h)] = jnp.transpose(turned)

    hop((5, 6))

    def mm(a, b):
        return jnp.dot(a, b, preferred_element_type=F32)

    def pick(is_low, low_rows, high_rows):
        return jnp.where(is_low, low_rows, high_rows)

    def key_rows(half, slot):
        span = low_ref[slot] if half == LOW else SPANS - 1 - low_ref[slot]
        cos, sin = rope_tables(span)
        part = kv[half, slot, KEY].astype(F32)
        part = part * spread(inv_buf[slot, 2 + half:3 + half, :]) * k_gain_row()
        part = part * cos + pltpu.roll(part, DH // 2, 1) * sin
        kr[half, slot] = part.astype(BF16)

    def values_pass(slot):
        is_low = sel_ref[slot] == 1
        other = 1 - sel_ref[slot]
        v_low = kv[LOW, slot, VAL]
        v_other = pick(is_low, v_low, kv[HIGH, slot, VAL])
        for start, width in CHUNKS:
            cols = pl.ds(start, width)
            dp_a[slot, :, cols] = mm(v_low, dot_[HIGH, :, cols])
            dp_b[slot, :, cols] = mm(v_other, dot_[other, :, cols])

    def scores(keys, half, cols, d_probs, exps, slot, mask=None):
        s = mm(keys, qt[half, :, cols])
        if mask is not None:
            s = jnp.where(mask, s, NEG)
        top = jnp.max(s, axis=0, keepdims=True)
        e = jnp.exp2(s * C2 - top * C2)
        exps[slot, :, cols] = e
        return (
            top,
            jnp.sum(e, axis=0, keepdims=True),
            jnp.sum(e * d_probs[slot, :, cols], axis=0, keepdims=True),
        )

    def put(tabs, row, cols, stats):
        for tab, value in zip(tabs, stats):
            tab[row, :, cols] = value

    tabs_high, tabs_low = (mh, lh, dh), (ml, ll, dl)

    def keys_pass(slot):
        chosen = sel_ref[slot]
        is_low = chosen == 1
        for half in (LOW, HIGH):
            key_rows(half, slot)
        k_low = kr[LOW, slot]
        k_other = pick(is_low, k_low, kr[HIGH, slot])
        for start, width in CHUNKS:
            cols = pl.ds(start, width)
            put(tabs_high, slot, cols, scores(k_low, HIGH, cols, dp_a, e_a, slot))
            top, total, dots = scores(k_other, 1 - chosen, cols, dp_b, e_b, slot)
            put(tabs_high, slot + 15, cols, (jnp.where(is_low, NEG, top), total, dots))
            put(tabs_low, slot, cols, (jnp.where(is_low, top, NEG), total, dots))

    def own_values():
        for start, width in CHUNKS:
            cols = pl.ds(start, width)
            dp_a[0, :, cols] = mm(kv[LOW, 0, VAL], dot_[HIGH, :, cols])
            dp_b[0, :, cols] = mm(kv[LOW, 0, VAL], dot_[LOW, :, cols])
            dp_b[16, :, cols] = mm(kv[HIGH, 0, VAL], dot_[HIGH, :, cols])

    def own_keys():
        for start, width in CHUNKS:
            cols = pl.ds(start, width)
            shape = (SPAN, width)
            mask = lax.broadcasted_iota(jnp.int32, shape, 0) <= (
                lax.broadcasted_iota(jnp.int32, shape, 1) % SPAN
            )
            put(tabs_high, 0, cols, scores(kr[LOW, 0], HIGH, cols, dp_a, e_a, 0))
            put(tabs_low, 0, cols, scores(kr[LOW, 0], LOW, cols, dp_b, e_b, 0, mask))
            put(tabs_high, 31, cols, scores(kr[HIGH, 0], HIGH, cols, dp_b, e_b, 16, mask))

    def each(step, slots):
        for slot in slots:
            step(slot)

    own_values()
    own_keys()
    each(values_pass, (1, 2, 3, 4))
    hop((7, 8, 9))
    each(values_pass, (5, 6))
    finished(inv_buf.at[pl.ds(1, SLOTS - 1)], small_sem.at[0])
    each(keys_pass, (1, 2, 3, 4, 5, 6))
    rest(10)
    each(values_pass, (7, 8, 9, 10, 11, 12))
    each(keys_pass, (7, 8, 9, 10, 11, 12))
    rest(13)
    each(values_pass, (13, 14, 15))
    each(keys_pass, (13, 14, 15))

    def finish(tabs, factors, half):
        tops, sums, dots = (tab[...] for tab in tabs)
        weights = jnp.exp2((tops - jnp.max(tops, axis=0, keepdims=True)) * C2)
        scale = 1.0 / jnp.sum(weights * sums, axis=0, keepdims=True)
        delta[half] = (jnp.sum(weights * dots, axis=0, keepdims=True) * scale)[0]
        factors[...] = weights * scale

    finish(tabs_high, fh, HIGH)
    finish(tabs_low, fl, LOW)

    def grads(exps, d_probs, slot, factor, shift, where):
        for start, width in CHUNKS:
            cols = pl.ds(start, width)
            probs = exps[slot, :, cols] * factor(cols)
            d_scores = probs * (d_probs[slot, :, cols] - shift(cols))
            pb[where, :, cols] = probs.astype(BF16)
            dsb[pl.ds(where * SPAN, SPAN), cols] = d_scores.astype(BF16)

    def rows(where):
        return pl.ds(where * SPAN, SPAN)

    def second_pass(slot):
        chosen = sel_ref[slot]
        is_low = chosen == 1
        other = 1 - chosen
        grads(e_a, dp_a, slot, lambda c: fh[slot, :, c], lambda c: delta[HIGH, :, c], 0)
        grads(
            e_b, dp_b, slot,
            lambda c: fl[slot, :, c] + fh[slot + 15, :, c],
            lambda c: delta[other, :, c], 1,
        )
        for kind, left in ((0, None), (1, None)):
            a_rows = pb[0] if kind == 0 else dsb[rows(0), :]
            b_rows = pb[1] if kind == 0 else dsb[rows(1), :]
            source = dos if kind == 0 else qs
            from_a = mm(a_rows, source[HIGH])
            from_b = mm(b_rows, source[other])
            cb[slot, LOW, kind] = from_a + jnp.where(is_low, from_b, 0.0)
            cb[slot, HIGH, kind] = jnp.where(is_low, 0.0, from_b)
        turned_low = jnp.transpose(kr[LOW, slot])
        turned_other = jnp.transpose(pick(is_low, kr[LOW, slot], kr[HIGH, slot]))
        none = jnp.zeros_like(turned_other)
        both = jnp.concatenate([turned_low, jnp.where(is_low, none, turned_other)], axis=1)
        only_low = jnp.where(is_low, turned_other, none)
        for start, width in CHUNKS:
            cols = pl.ds(start, width)
            acc[HIGH, :, cols] += mm(both, dsb[0:2 * SPAN, cols])
            acc[LOW, :, cols] += mm(only_low, dsb[rows(1), cols])

    def own_second():
        grads(e_a, dp_a, 0, lambda c: fh[0, :, c], lambda c: delta[HIGH, :, c], 0)
        grads(e_b, dp_b, 16, lambda c: fh[31, :, c], lambda c: delta[HIGH, :, c], 1)
        grads(e_b, dp_b, 0, lambda c: fl[0, :, c], lambda c: delta[LOW, :, c], 2)
        for kind in (0, 1):
            source = dos if kind == 0 else qs
            parts = [pb[i] if kind == 0 else dsb[rows(i), :] for i in range(3)]
            cb[0, LOW, kind] = mm(parts[0], source[HIGH]) + mm(parts[2], source[LOW])
            cb[0, HIGH, kind] = mm(parts[1], source[HIGH])
        turned_low = jnp.transpose(kr[LOW, 0])
        turned_high = jnp.transpose(kr[HIGH, 0])
        both = jnp.concatenate([turned_low, turned_high], axis=1)
        for start, width in CHUNKS:
            cols = pl.ds(start, width)
            acc[HIGH, :, cols] += mm(both, dsb[0:2 * SPAN, cols])
            acc[LOW, :, cols] += mm(turned_low, dsb[rows(2), cols])

    acc[...] = jnp.zeros_like(acc)

    PLACE = {1: 1, 3: 2, 2: 3}

    def ring_copy(half, first, place):
        step = {1: 1, 2: 3, 3: 1 if first else 2}[place]
        return pltpu.make_async_remote_copy(
            src_ref=stage.at[half, first, place],
            dst_ref=gotr.at[half, first, place],
            send_sem=sent.at[1],
            recv_sem=(far_sem if first and place == 3 else rs_sem).at[half, first],
            device_id=neighbour(half, 1, step),
            device_id_type=pl.DeviceIdType.MESH,
        )

    def last_copy(half, first):
        return pltpu.make_async_remote_copy(
            src_ref=pstage.at[half, first],
            dst_ref=gotp.at[half, first],
            send_sem=sent.at[2],
            recv_sem=ps_sem.at[half],
            device_id=neighbour(half, 0, first),
            device_id_type=pl.DeviceIdType.MESH,
        )

    def ring_send(half, slot):
        first, second = primary_view(half, slot)
        if second > 1 or (second == 1 and first == 0):
            stage[half, first, PLACE[second]] = cb[slot, half].astype(BF16)
            ring_copy(half, first, PLACE[second]).start()

    def near_send(first):
        for half in (LOW, HIGH):
            ring_copy(half, first, 3).wait_recv()
            mixed = cb[slot_of(half, first, 1), half] + gotr[half, first, 3].astype(F32)
            stage[half, first, 1] = mixed.astype(BF16)
            ring_copy(half, first, 1).start()

    def ring_sum(half, first):
        count = 2 if first else 3
        finished(gotr.at[half, first, pl.ds(1, count)], rs_sem.at[half, first])
        total = cb[slot_of(half, first, 0), half]
        for place in range(1, count + 1):
            total = total + gotr[half, first, place].astype(F32)
        return total

    def gain_part(half, first, d_rot):
        slot = slot_of(half, first, 0)
        span = low_ref[slot] if half == LOW else SPANS - 1 - low_ref[slot]
        cos, sin = rope_tables(span)
        d_norm = d_rot * cos - pltpu.roll(d_rot, DH // 2, 1) * sin
        k_hat = kv[half, slot, KEY].astype(F32) * spread(inv_buf[slot, 2 + half:3 + half, :])
        gain_buf[0, 5:6, :] += jnp.sum(d_norm * k_hat, axis=0, keepdims=True)

    def last_send(first):
        totals = []
        for half in (LOW, HIGH):
            totals.append(ring_sum(half, first))
            pstage[half, first] = totals[half].astype(BF16)
            last_copy(half, first).start()
        for half in (LOW, HIGH):
            gain_part(half, first, totals[half][1] * SCALE)

    steps = (15, 14, 13, 12, 11, 7, 9, 8, 6, 5, 10, 4, 3, 2, 1)
    near = {10: 2, 4: 1, 2: 3}
    for slot in steps:
        second_pass(slot)
        for half in (LOW, HIGH):
            ring_send(half, slot)
        if slot in near:
            near_send(near[slot])
    own_second()

    stat[1, 0] = jnp.zeros((8, SPAN), F32)
    gain_buf[0] = jnp.zeros((8, DH), F32)
    for half in (LOW, HIGH):
        inner = jnp.zeros((SPAN, DH), F32)
        for h in range(GROUP):
            d_rot = jnp.transpose(acc[half, :, head(h)]) * SCALE
            d_norm = rotated(half, d_rot, -1)
            q_hat = q_ref[offs[half], :, head(h)].astype(F32) * qi[half]
            gain_buf[0, h:h + 1, :] += jnp.sum(d_norm * q_hat, axis=0, keepdims=True)
            scaled = d_norm * q_gain_row(h)
            sg[half, :, head(h)] = scaled
            inner = inner + scaled * q_hat
        stat[1, 0, half:half + 1, :] = token_sums(inner)
    stat_send(1)

    for first in (2, 1, 3):
        last_send(first)

    q_inner = stat_total(1) / D
    for half in (LOW, HIGH):
        inner = spread(q_inner[half:half + 1, :])
        for h in range(GROUP):
            q_hat = q_ref[offs[half], :, head(h)].astype(F32) * qi[half]
            sg[half, :, head(h)] = qi[half] * (sg[half, :, head(h)] - q_hat * inner)

    first_half = jnp.where(s0 < s1, LOW, HIGH)
    places = ((0, first_half), (1, 1 - first_half))
    for place, half in places:
        dq_out[place * SPAN:(place + 1) * SPAN, :] = sg[half].astype(BF16)

    def store(number, source, target):
        return pltpu.make_async_copy(source, target, out_sem.at[number])

    stores = [
        store(number, source, target)
        for number, (source, target) in enumerate(
            (
                (dq_out, dq_hbm), (dk_out, dk_hbm), (dv_out, dv_hbm),
                (dqg_out, dqg_hbm), (dkg_out, dkg_hbm),
            )
        )
    ]
    stores[0].start()

    totals = [ring_sum(half, 0) for half in (LOW, HIGH)]
    for half in (LOW, HIGH):
        gain_part(half, 0, totals[half][1] * SCALE)

    def gain_copy(slot):
        return pltpu.make_async_remote_copy(
            src_ref=gain_buf.at[0],
            dst_ref=gain_buf.at[slot],
            send_sem=sent.at[5],
            recv_sem=small_sem.at[1],
            device_id=to_ctx(ORDER[slot]),
            device_id_type=pl.DeviceIdType.MESH,
        )

    for slot in range(SLOTS - 1, 0, -1):
        gain_copy(slot).start()

    stat[2, 0] = jnp.zeros((8, SPAN), F32)
    for half in (LOW, HIGH):
        finished(gotp.at[half, pl.ds(1, 3)], ps_sem.at[half])
        total = totals[half]
        for first in (2, 1, 3):
            total = total + gotp[half, first].astype(F32)
        dkn[1, half] = total[0]
        d_norm = rotated(half, total[1] * SCALE, -1)
        k_hat = kv[half, 0, KEY].astype(F32) * ki[half]
        scaled = d_norm * k_gain_row()
        dkn[0, half] = scaled
        stat[2, 0, half:half + 1, :] = token_sums(scaled * k_hat)
    stat_send(2)

    for place, half in places:
        dv_out[place * SPAN:(place + 1) * SPAN, :] = dkn[1, half].astype(BF16)
    stores[2].start()

    k_inner = stat_total(2) / KVD
    for half in (LOW, HIGH):
        inner = spread(k_inner[half:half + 1, :])
        k_hat = kv[half, 0, KEY].astype(F32) * ki[half]
        dkn[0, half] = ki[half] * (dkn[0, half] - k_hat * inner)
    for place, half in places:
        dk_out[place * SPAN:(place + 1) * SPAN, :] = dkn[0, half].astype(BF16)
    stores[1].start()

    finished(gain_buf.at[pl.ds(1, SLOTS - 1)], small_sem.at[1])
    total = gain_buf[0]
    for slot in range(1, SLOTS):
        total = total + gain_buf[slot]
    for h in range(GROUP):
        dqg_out[head(h)] = total[h:h + 1, :].reshape(DH)
    dkg_out[...] = total[5:6, :].reshape(DH)
    stores[3].start()
    stores[4].start()

    finished(kv.at[:, pl.ds(0, SLOTS - 1)], sent.at[0])
    finished(stage.at[:, :, pl.ds(1, 3)], sent.at[1])
    finished(pstage.at[:, pl.ds(1, 3)], sent.at[2])
    finished(stat.at[:, pl.ds(1, 7)], sent.at[3])
    finished(inv_buf.at[pl.ds(1, SLOTS - 1)], sent.at[4])
    finished(gain_buf.at[pl.ds(1, SLOTS - 1)], sent.at[5])
    for item in stores:
        item.wait()


def pass_on(*refs):
    for source, target in zip(refs[:5], refs[5:]):
        target[...] = source[...]


def per_device(q_raw, k_raw, values, d_out, q_gain, k_gain, span_order):
    token_table, span_table = tables()
    tile = (SPAN, DH)
    dma = pltpu.SemaphoreType.DMA
    wide = (SPAN, QW)
    scratch = [
        pltpu.SMEM((SPANS,), jnp.int32),
        pltpu.VMEM((QW,), F32), pltpu.VMEM((DH,), F32),
        pltpu.VMEM((2,) + tile, F32), pltpu.VMEM((2, SPANS, 1, DH), F32),
        pltpu.VMEM((2 * SPAN, QW), BF16), pltpu.VMEM((2 * SPAN, DH), BF16),
        pltpu.VMEM((2 * SPAN, DH), BF16), pltpu.VMEM((QW,), F32), pltpu.VMEM((DH,), F32),
        pltpu.SMEM((SLOTS,), jnp.int32),
        pltpu.SMEM((SLOTS,), jnp.int32),
        pltpu.VMEM((2,) + wide, BF16),
        pltpu.VMEM((2,) + tile, BF16),
        pltpu.VMEM((2,) + tile, BF16),
        pltpu.VMEM((2,) + wide, BF16),
        pltpu.VMEM((2, SLOTS, 2) + tile, BF16),
        pltpu.VMEM((2, SLOTS) + tile, BF16),
        pltpu.VMEM((2, QW, DH), BF16),
        pltpu.VMEM((2, DH, QW), BF16),
        pltpu.VMEM((2, QW, DH), BF16),
        pltpu.VMEM((2, DH, QW), BF16),
        pltpu.VMEM((2, 2) + tile, F32),
        pltpu.VMEM((2,) + tile, F32),
        pltpu.VMEM((2,) + tile, F32),
        pltpu.VMEM((16,) + wide, F32),
        pltpu.VMEM((17,) + wide, F32),
        pltpu.VMEM((16,) + wide, F32),
        pltpu.VMEM((17,) + wide, F32),
        pltpu.VMEM((32, 1, QW), F32),
        pltpu.VMEM((32, 1, QW), F32),
        pltpu.VMEM((32, 1, QW), F32),
        pltpu.VMEM((16, 1, QW), F32),
        pltpu.VMEM((16, 1, QW), F32),
        pltpu.VMEM((16, 1, QW), F32),
        pltpu.VMEM((32, 1, QW), F32),
        pltpu.VMEM((16, 1, QW), F32),
        pltpu.VMEM((2, 1, QW), F32),
        pltpu.VMEM((3,) + wide, BF16),
        pltpu.VMEM((3 * SPAN, QW), BF16),
        pltpu.VMEM((2,) + wide, F32),
        pltpu.VMEM((SLOTS, 2, 2) + tile, F32),
        pltpu.VMEM((2, RING, RING, 2) + tile, BF16),
        pltpu.VMEM((2, RING, RING, 2) + tile, BF16),
        pltpu.VMEM((2, RING, 2) + tile, BF16),
        pltpu.VMEM((2, RING, 2) + tile, BF16),
        pltpu.VMEM((2,) + wide, F32),
        pltpu.VMEM((2, 2) + tile, F32),
        pltpu.VMEM((3, 8, 8, SPAN), F32),
        pltpu.VMEM((SLOTS, 8, SPAN), F32),
        pltpu.VMEM((SLOTS, 8, DH), F32),
        dma((9,)), dma((5,)), pltpu.SemaphoreType.REGULAR,
        dma((6,)),
        dma((2, 10)), dma((2,)),
        dma((2, RING)), dma((2, RING)),
        dma((2,)), dma((3,)), dma((2,)),
    ]
    rows = 2 * SPAN
    shapes = (
        jax.ShapeDtypeStruct((rows, QW), BF16),
        jax.ShapeDtypeStruct((rows, DH), BF16),
        jax.ShapeDtypeStruct((rows, DH), BF16),
        jax.ShapeDtypeStruct((QW,), F32),
        jax.ShapeDtypeStruct((DH,), F32),
    )
    vmem = pl.BlockSpec(memory_space=pltpu.VMEM)
    hbm = pl.BlockSpec(memory_space=pltpu.HBM)
    results = pl.pallas_call(
        kernel,
        out_shape=shapes,
        in_specs=[hbm] * 9,
        out_specs=(hbm,) * 5,
        scratch_shapes=scratch,
        compiler_params=pltpu.CompilerParams(
            collective_id=0, has_side_effects=True, vmem_limit_bytes=60 * 2**20
        ),
    )(
        span_order,
        q_raw.reshape(2, SPAN, QW), k_raw.reshape(2, SPAN, DH),
        values.reshape(2, SPAN, DH), d_out.reshape(2, SPAN, QW),
        q_gain, k_gain, token_table, span_table,
    )
    return pl.pallas_call(
        pass_on, out_shape=shapes, in_specs=[vmem] * 5, out_specs=(vmem,) * 5,
        compiler_params=pltpu.CompilerParams(vmem_limit_bytes=60 * 2**20),
    )(*results)


def solution(mesh):
    return jax.shard_map(
        per_device,
        mesh=mesh,
        in_specs=(
            P("ctx", "tp"),
            P("ctx", "tp"),
            P("ctx", "tp"),
            P("ctx", "tp"),
            P("tp"),
            P("tp"),
            P(),
        ),
        out_specs=(P("ctx", "tp"), P("ctx", "tp"), P("ctx", "tp"), P("tp"), P("tp")),
        check_vma=False,
    )
```

```python
import math

import jax
import jax.numpy as jnp
import numpy as np
from jax import lax
from jax.experimental import pallas as pl
from jax.experimental.pallas import tpu as pltpu
from jax.sharding import PartitionSpec as P

D = 5120
KVD = 1024
DH = 128
SPAN = 128
SPANS = 32
GROUP = 5
QW = GROUP * DH
EPS = 1e-06
THETA = 500000.0
NEG = -1e30
SCALE = DH ** (-0.5)
C2 = SCALE * math.log2(math.e)
RING = 4
SLOTS = 16
F32 = jnp.float32
BF16 = jnp.bfloat16

ORDER = [
    (0, 0), (0, 3), (3, 0), (0, 1), (1, 0), (0, 2), (2, 0), (3, 3),
    (1, 3), (3, 1), (1, 1), (3, 2), (2, 3), (1, 2), (2, 1), (2, 2),
]
SLOT = {pair: number for number, pair in enumerate(ORDER)}
MIRROR = [SLOT[(-oz % RING, -ox % RING)] for oz, ox in ORDER]
RINGS = [(0, 1), (0, 2), (0, 3), (1, 0), (2, 0), (3, 0)]
CHUNKS = ((0, 256), (256, 256), (512, 128))
LOW, HIGH = 0, 1
KEY, VAL = 0, 1


def primary_view(half, slot):
    oz, ox = ORDER[slot]
    return (ox, oz) if half == LOW else (oz, ox)


def slot_of(half, first, second):
    return SLOT[(second, first)] if half == LOW else SLOT[(first, second)]


def gather_sends(half, slot):
    first, second = primary_view(half, slot)
    sends = []
    if second == 0:
        if first == 0:
            sends += [(0, step, slot_of(half, -step % RING, 0)) for step in (1, 3, 2)]
        sends += [(1, step, slot_of(half, first, -step % RING)) for step in (1, 3)]
        if first == 2:
            sends += [(1, 2, slot_of(half, first, 2))]
    if second == 3 and first != 2:
        sends += [(1, 1, slot_of(half, first, 2))]
    return sends


def tables():
    freq = np.asarray(
        np.float32(THETA) ** (-np.arange(DH // 2, dtype=np.float32) / np.float32(DH // 2)),
        np.float64,
    )
    sign = np.concatenate([-np.ones(DH // 2), np.ones(DH // 2)])

    def pair(numbers):
        angle = np.asarray(numbers, np.float64)[:, None] * freq[None, :]
        cos = np.concatenate([np.cos(angle)] * 2, axis=1)
        sin = np.concatenate([np.sin(angle)] * 2, axis=1) * sign
        return cos, sin

    cos_t, sin_t = pair(np.arange(SPAN))
    cos_s, sin_s = pair(np.arange(SPANS) * SPAN)
    token = np.stack([cos_t, sin_t]).astype(np.float32)
    span = np.stack([cos_s, sin_s])[:, :, None, :].astype(np.float32)
    return jnp.asarray(token), jnp.asarray(span)


def kernel(
    so_in, q_in, k_in, v_in, do_in, qg_in, kg_in, tab_in, span_in,
    dq_hbm, dk_hbm, dv_hbm, dqg_hbm, dkg_hbm,
    so_ref, qg_ref, kg_ref, tab_ref, span_ref, dq_out, dk_out, dv_out, dqg_out, dkg_out,
    sel_ref, low_ref, q_ref, k_ref, v_ref, do_ref,
    kv, kr, qs, qt, dos, dot_, rope, qi, ki,
    e_a, e_b, dp_a, dp_b, mh, lh, dh, ml, ll, dl, fh, fl, delta,
    pb, dsb, acc, cb, stage, gotr, pstage, gotp, sg, dkn,
    stat, inv_buf, gain_buf,
    in_sem, out_sem, relay, sent, ag_sem, rest_sem, far_sem, rs_sem, ps_sem, st_sem, small_sem,
):
    order_load = pltpu.make_async_copy(so_in, so_ref, in_sem.at[8])
    order_load.start()
    loads = [
        pltpu.make_async_copy(source, target, in_sem.at[number])
        for number, (source, target) in enumerate(
            (
                (k_in, k_ref), (v_in, v_ref), (q_in, q_ref), (do_in, do_ref),
                (qg_in, qg_ref), (kg_in, kg_ref), (tab_in, tab_ref), (span_in, span_ref),
            )
        )
    ]
    for load in loads:
        load.start()

    ctx = lax.axis_index("ctx")
    tp = lax.axis_index("tp")
    z, x = ctx // RING, ctx % RING
    flip = tp % 2
    turned_z = [z] + [(z + jnp.where(flip == 0, o, RING - o)) % RING for o in (1, 2, 3)]
    turned_x = [x] + [(x + jnp.where(flip == 0, o, RING - o)) % RING for o in (1, 2, 3)]
    peers = {(oz, ox): turned_z[oz] * RING + turned_x[ox] for oz, ox in ORDER}
    tp_peers = [(tp + offset) % 8 for offset in range(8)]

    def to_ctx(pair):
        return {"ctx": peers[pair]}

    barrier = pltpu.get_barrier_semaphore()
    for pair in RINGS:
        pl.semaphore_signal(
            barrier, inc=1, device_id=to_ctx(pair), device_id_type=pl.DeviceIdType.MESH
        )
    for offset in range(1, 8):
        pl.semaphore_signal(
            barrier, inc=1, device_id={"tp": tp_peers[offset]},
            device_id_type=pl.DeviceIdType.MESH,
        )

    order_load.wait()
    s0, s1 = so_ref[2 * ctx], so_ref[2 * ctx + 1]
    low = jnp.minimum(s0, s1)
    offs = (jnp.where(s0 < s1, 0, 1), jnp.where(s0 < s1, 1, 0))
    low_ref[0] = low
    for slot in range(1, SLOTS):
        other = peers[ORDER[slot]]
        a = jnp.minimum(so_ref[2 * other], so_ref[2 * other + 1])
        low_ref[slot] = a
        sel_ref[slot] = jnp.where(a < low, 1, 0)

    loads[0].wait()
    loads[1].wait()
    for half in (LOW, HIGH):
        kv[half, 0, KEY] = k_ref[offs[half]]
        kv[half, 0, VAL] = v_ref[offs[half]]

    pl.semaphore_wait(barrier, 13)

    axis_of = {LOW: ("x", "z"), HIGH: ("z", "x")}

    def neighbour(half, axis, step):
        return to_ctx((step, 0) if axis_of[half][axis] == "z" else (0, step))

    def gather_arrival(half, dst):
        if dst < 10:
            return ag_sem.at[half, dst]
        return rest_sem.at[0 if dst < 13 else 1]

    def gather_copy(half, slot, axis, step, dst):
        return pltpu.make_async_remote_copy(
            src_ref=kv.at[half, slot],
            dst_ref=kv.at[half, dst],
            send_sem=sent.at[0],
            recv_sem=gather_arrival(half, dst),
            device_id=neighbour(half, axis, step),
            device_id_type=pl.DeviceIdType.MESH,
        )

    def gather_forward(half, slot):
        for axis, step, dst in gather_sends(half, slot):
            gather_copy(half, slot, axis, step, dst).start()

    def hop(slots):
        for slot in slots:
            for half in (LOW, HIGH):
                gather_copy(half, slot, 0, 1, slot).wait_recv()
                gather_forward(half, slot)

    def finished(block, sem):
        pltpu.make_async_copy(block, block, sem).wait()

    def rest(first):
        finished(kv.at[:, pl.ds(first, 3)], rest_sem.at[0 if first < 13 else 1])

    gather_forward(LOW, 0)
    gather_forward(HIGH, 0)
    for pair in RINGS[3:]:
        pl.semaphore_signal(
            relay, inc=1, device_id=to_ctx(pair), device_id_type=pl.DeviceIdType.MESH
        )

    def stat_copy(kind, offset):
        return pltpu.make_async_remote_copy(
            src_ref=stat.at[kind, 0],
            dst_ref=stat.at[kind, offset],
            send_sem=sent.at[3],
            recv_sem=st_sem.at[kind],
            device_id={"tp": tp_peers[offset]},
            device_id_type=pl.DeviceIdType.MESH,
        )

    def stat_send(kind):
        for offset in range(1, 8):
            stat_copy(kind, offset).start()

    def stat_total(kind):
        finished(stat.at[kind, pl.ds(1, 7)], st_sem.at[kind])
        total = stat[kind, 0]
        for offset in range(1, 8):
            total = total + stat[kind, offset]
        return total

    def token_sums(square):
        return jnp.sum(jnp.transpose(square), axis=0, keepdims=True)

    def spread(row):
        return jnp.transpose(jnp.broadcast_to(row, (SPAN, SPAN)))

    def head(number):
        return slice(number * DH, (number + 1) * DH)

    def q_gain_row(h):
        return qg_ref[head(h)].reshape(1, DH)

    def k_gain_row():
        return kg_ref[...].reshape(1, DH)

    for load in loads[2:]:
        load.wait()
    stat[0, 0] = jnp.zeros((8, SPAN), F32)
    for half in (LOW, HIGH):
        square = jnp.zeros((SPAN, DH), F32)
        for h in range(GROUP):
            part = q_ref[offs[half], :, head(h)].astype(F32)
            square = square + part * part
        stat[0, 0, half:half + 1, :] = token_sums(square)
        part = kv[half, 0, KEY].astype(F32)
        stat[0, 0, 2 + half:3 + half, :] = token_sums(part * part)
    stat_send(0)

    def rope_tables(span):
        cos_t, sin_t = tab_ref[0], tab_ref[1]
        cos_s, sin_s = span_ref[0, span], span_ref[1, span]
        return cos_s * cos_t - sin_s * sin_t, sin_s * cos_t + cos_s * sin_t

    for half, span in ((LOW, low), (HIGH, SPANS - 1 - low)):
        rope[half, 0], rope[half, 1] = rope_tables(span)
    for half in (LOW, HIGH):
        for h in range(GROUP):
            part = do_ref[offs[half], :, head(h)]
            dos[half, head(h), :] = part
            dot_[half, :, head(h)] = jnp.transpose(part)

    def rotated(half, part, sign):
        turned = pltpu.roll(part, DH // 2, 1) * rope[half, 1]
        straight = part * rope[half, 0]
        return straight + turned if sign > 0 else straight - turned

    total = stat_total(0)
    pl.semaphore_wait(relay, 3)
    inv_buf[0] = lax.rsqrt(total / KVD + EPS)
    q_inv = lax.rsqrt(total / D + EPS)

    def inv_copy(slot):
        return pltpu.make_async_remote_copy(
            src_ref=inv_buf.at[0],
            dst_ref=inv_buf.at[MIRROR[slot]],
            send_sem=sent.at[4],
            recv_sem=small_sem.at[0],
            device_id=to_ctx(ORDER[slot]),
            device_id_type=pl.DeviceIdType.MESH,
        )

    for slot in range(1, SLOTS):
        inv_copy(slot).start()

    hop((1, 2, 3, 4))

    for half in (LOW, HIGH):
        ki[half] = spread(inv_buf[0, 2 + half:3 + half, :])
        part = kv[half, 0, KEY].astype(F32) * ki[half] * k_gain_row()
        kr[half, 0] = rotated(half, part, 1).astype(BF16)
        qi[half] = spread(q_inv[half:half + 1, :])
        for h in range(GROUP):
            part = q_ref[offs[half], :, head(h)].astype(F32) * qi[half] * q_gain_row(h)
            turned = rotated(half, part, 1).astype(BF16)
            qs[half, head(h), :] = turned
            qt[half, :, head(h)] = jnp.transpose(turned)

    hop((5, 6))

    def mm(a, b):
        return jnp.dot(a, b, preferred_element_type=F32)

    def pick(is_low, low_rows, high_rows):
        return jnp.where(is_low, low_rows, high_rows)

    def key_rows(half, slot):
        span = low_ref[slot] if half == LOW else SPANS - 1 - low_ref[slot]
        cos, sin = rope_tables(span)
        part = kv[half, slot, KEY].astype(F32)
        part = part * spread(inv_buf[slot, 2 + half:3 + half, :]) * k_gain_row()
        part = part * cos + pltpu.roll(part, DH // 2, 1) * sin
        kr[half, slot] = part.astype(BF16)

    def values_pass(slot):
        is_low = sel_ref[slot] == 1
        other = 1 - sel_ref[slot]
        v_low = kv[LOW, slot, VAL]
        v_other = pick(is_low, v_low, kv[HIGH, slot, VAL])
        for start, width in CHUNKS:
            cols = pl.ds(start, width)
            dp_a[slot, :, cols] = mm(v_low, dot_[HIGH, :, cols])
            dp_b[slot, :, cols] = mm(v_other, dot_[other, :, cols])

    def scores(keys, half, cols, d_probs, exps, slot, mask=None):
        s = mm(keys, qt[half, :, cols])
        if mask is not None:
            s = jnp.where(mask, s, NEG)
        top = jnp.max(s, axis=0, keepdims=True)
        e = jnp.exp2(s * C2 - top * C2)
        exps[slot, :, cols] = e
        return (
            top,
            jnp.sum(e, axis=0, keepdims=True),
            jnp.sum(e * d_probs[slot, :, cols], axis=0, keepdims=True),
        )

    def put(tabs, row, cols, stats):
        for tab, value in zip(tabs, stats):
            tab[row, :, cols] = value

    tabs_high, tabs_low = (mh, lh, dh), (ml, ll, dl)

    def keys_pass(slot):
        chosen = sel_ref[slot]
        is_low = chosen == 1
        for half in (LOW, HIGH):
            key_rows(half, slot)
        k_low = kr[LOW, slot]
        k_other = pick(is_low, k_low, kr[HIGH, slot])
        for start, width in CHUNKS:
            cols = pl.ds(start, width)
            put(tabs_high, slot, cols, scores(k_low, HIGH, cols, dp_a, e_a, slot))
            top, total, dots = scores(k_other, 1 - chosen, cols, dp_b, e_b, slot)
            put(tabs_high, slot + 15, cols, (jnp.where(is_low, NEG, top), total, dots))
            put(tabs_low, slot, cols, (jnp.where(is_low, top, NEG), total, dots))

    def own_values():
        for start, width in CHUNKS:
            cols = pl.ds(start, width)
            dp_a[0, :, cols] = mm(kv[LOW, 0, VAL], dot_[HIGH, :, cols])
            dp_b[0, :, cols] = mm(kv[LOW, 0, VAL], dot_[LOW, :, cols])
            dp_b[16, :, cols] = mm(kv[HIGH, 0, VAL], dot_[HIGH, :, cols])

    def own_keys():
        for start, width in CHUNKS:
            cols = pl.ds(start, width)
            shape = (SPAN, width)
            mask = lax.broadcasted_iota(jnp.int32, shape, 0) <= (
                lax.broadcasted_iota(jnp.int32, shape, 1) % SPAN
            )
            put(tabs_high, 0, cols, scores(kr[LOW, 0], HIGH, cols, dp_a, e_a, 0))
            put(tabs_low, 0, cols, scores(kr[LOW, 0], LOW, cols, dp_b, e_b, 0, mask))
            put(tabs_high, 31, cols, scores(kr[HIGH, 0], HIGH, cols, dp_b, e_b, 16, mask))

    def each(step, slots):
        for slot in slots:
            step(slot)

    own_values()
    own_keys()
    each(values_pass, (1, 2, 3, 4))
    hop((7, 8, 9))
    each(values_pass, (5, 6))
    finished(inv_buf.at[pl.ds(1, SLOTS - 1)], small_sem.at[0])
    each(keys_pass, (1, 2, 3, 4, 5, 6))
    rest(10)
    each(values_pass, (7, 8, 9, 10, 11, 12))
    each(keys_pass, (7, 8, 9, 10, 11, 12))
    rest(13)
    each(values_pass, (13, 14, 15))
    each(keys_pass, (13, 14, 15))

    def finish(tabs, factors, half):
        tops, sums, dots = (tab[...] for tab in tabs)
        weights = jnp.exp2((tops - jnp.max(tops, axis=0, keepdims=True)) * C2)
        scale = 1.0 / jnp.sum(weights * sums, axis=0, keepdims=True)
        delta[half] = (jnp.sum(weights * dots, axis=0, keepdims=True) * scale)[0]
        factors[...] = weights * scale

    finish(tabs_high, fh, HIGH)
    finish(tabs_low, fl, LOW)

    def grads(exps, d_probs, slot, factor, shift, where):
        for start, width in CHUNKS:
            cols = pl.ds(start, width)
            probs = exps[slot, :, cols] * factor(cols)
            d_scores = probs * (d_probs[slot, :, cols] - shift(cols))
            pb[where, :, cols] = probs.astype(BF16)
            dsb[pl.ds(where * SPAN, SPAN), cols] = d_scores.astype(BF16)

    def rows(where):
        return pl.ds(where * SPAN, SPAN)

    def second_pass(slot):
        chosen = sel_ref[slot]
        is_low = chosen == 1
        other = 1 - chosen
        grads(e_a, dp_a, slot, lambda c: fh[slot, :, c], lambda c: delta[HIGH, :, c], 0)
        grads(
            e_b, dp_b, slot,
            lambda c: fl[slot, :, c] + fh[slot + 15, :, c],
            lambda c: delta[other, :, c], 1,
        )
        for kind, left in ((0, None), (1, None)):
            a_rows = pb[0] if kind == 0 else dsb[rows(0), :]
            b_rows = pb[1] if kind == 0 else dsb[rows(1), :]
            source = dos if kind == 0 else qs
            from_a = mm(a_rows, source[HIGH])
            from_b = mm(b_rows, source[other])
            cb[slot, LOW, kind] = from_a + jnp.where(is_low, from_b, 0.0)
            cb[slot, HIGH, kind] = jnp.where(is_low, 0.0, from_b)
        turned_low = jnp.transpose(kr[LOW, slot])
        turned_other = jnp.transpose(pick(is_low, kr[LOW, slot], kr[HIGH, slot]))
        none = jnp.zeros_like(turned_other)
        both = jnp.concatenate([turned_low, jnp.where(is_low, none, turned_other)], axis=1)
        only_low = jnp.where(is_low, turned_other, none)
        for start, width in CHUNKS:
            cols = pl.ds(start, width)
            acc[HIGH, :, cols] += mm(both, dsb[0:2 * SPAN, cols])
            acc[LOW, :, cols] += mm(only_low, dsb[rows(1), cols])

    def own_second():
        grads(e_a, dp_a, 0, lambda c: fh[0, :, c], lambda c: delta[HIGH, :, c], 0)
        grads(e_b, dp_b, 16, lambda c: fh[31, :, c], lambda c: delta[HIGH, :, c], 1)
        grads(e_b, dp_b, 0, lambda c: fl[0, :, c], lambda c: delta[LOW, :, c], 2)
        for kind in (0, 1):
            source = dos if kind == 0 else qs
            parts = [pb[i] if kind == 0 else dsb[rows(i), :] for i in range(3)]
            cb[0, LOW, kind] = mm(parts[0], source[HIGH]) + mm(parts[2], source[LOW])
            cb[0, HIGH, kind] = mm(parts[1], source[HIGH])
        turned_low = jnp.transpose(kr[LOW, 0])
        turned_high = jnp.transpose(kr[HIGH, 0])
        both = jnp.concatenate([turned_low, turned_high], axis=1)
        for start, width in CHUNKS:
            cols = pl.ds(start, width)
            acc[HIGH, :, cols] += mm(both, dsb[0:2 * SPAN, cols])
            acc[LOW, :, cols] += mm(turned_low, dsb[rows(2), cols])

    acc[...] = jnp.zeros_like(acc)

    PLACE = {1: 1, 3: 2, 2: 3}

    def ring_copy(half, first, place):
        step = {1: 1, 2: 3, 3: 2 if first == 2 else 1}[place]
        return pltpu.make_async_remote_copy(
            src_ref=stage.at[half, first, place],
            dst_ref=gotr.at[half, first, place],
            send_sem=sent.at[1],
            recv_sem=(far_sem if first != 2 and place == 3 else rs_sem).at[half, first],
            device_id=neighbour(half, 1, step),
            device_id_type=pl.DeviceIdType.MESH,
        )

    def last_copy(half, first):
        return pltpu.make_async_remote_copy(
            src_ref=pstage.at[half, first],
            dst_ref=gotp.at[half, first],
            send_sem=sent.at[2],
            recv_sem=ps_sem.at[half],
            device_id=neighbour(half, 0, first),
            device_id_type=pl.DeviceIdType.MESH,
        )

    def ring_send(half, slot):
        first, second = primary_view(half, slot)
        if second > 1 or (second == 1 and first == 2):
            stage[half, first, PLACE[second]] = cb[slot, half].astype(BF16)
            ring_copy(half, first, PLACE[second]).start()

    def near_send(first):
        for half in (LOW, HIGH):
            ring_copy(half, first, 3).wait_recv()
            mixed = cb[slot_of(half, first, 1), half] + gotr[half, first, 3].astype(F32)
            stage[half, first, 1] = mixed.astype(BF16)
            ring_copy(half, first, 1).start()

    def ring_sum(half, first):
        count = 3 if first == 2 else 2
        finished(gotr.at[half, first, pl.ds(1, count)], rs_sem.at[half, first])
        total = cb[slot_of(half, first, 0), half]
        for place in range(1, count + 1):
            total = total + gotr[half, first, place].astype(F32)
        return total

    def gain_part(half, first, d_rot):
        slot = slot_of(half, first, 0)
        span = low_ref[slot] if half == LOW else SPANS - 1 - low_ref[slot]
        cos, sin = rope_tables(span)
        d_norm = d_rot * cos - pltpu.roll(d_rot, DH // 2, 1) * sin
        k_hat = kv[half, slot, KEY].astype(F32) * spread(inv_buf[slot, 2 + half:3 + half, :])
        gain_buf[0, 5:6, :] += jnp.sum(d_norm * k_hat, axis=0, keepdims=True)

    def last_send(first):
        totals = []
        for half in (LOW, HIGH):
            totals.append(ring_sum(half, first))
            pstage[half, first] = totals[half].astype(BF16)
            last_copy(half, first).start()
        return totals

    steps = (15, 14, 13, 12, 11, 7, 9, 8, 6, 5, 10, 4, 3, 2, 1)
    near = {4: 1, 2: 3}
    for slot in steps:
        second_pass(slot)
        for half in (LOW, HIGH):
            ring_send(half, slot)
        if slot in near:
            near_send(near[slot])
    own_second()
    partial = {2: last_send(2)}

    stat[1, 0] = jnp.zeros((8, SPAN), F32)
    gain_buf[0] = jnp.zeros((8, DH), F32)
    for half in (LOW, HIGH):
        inner = jnp.zeros((SPAN, DH), F32)
        for h in range(GROUP):
            d_rot = jnp.transpose(acc[half, :, head(h)]) * SCALE
            d_norm = rotated(half, d_rot, -1)
            q_hat = q_ref[offs[half], :, head(h)].astype(F32) * qi[half]
            gain_buf[0, h:h + 1, :] += jnp.sum(d_norm * q_hat, axis=0, keepdims=True)
            scaled = d_norm * q_gain_row(h)
            sg[half, :, head(h)] = scaled
            inner = inner + scaled * q_hat
        stat[1, 0, half:half + 1, :] = token_sums(inner)
    stat_send(1)

    near_send(0)
    for first in (1, 3):
        partial[first] = last_send(first)

    first_half = jnp.where(s0 < s1, LOW, HIGH)
    places = ((0, first_half), (1, 1 - first_half))
    def store(number, source, target):
        return pltpu.make_async_copy(source, target, out_sem.at[number])

    stores = [
        store(number, source, target)
        for number, (source, target) in enumerate(
            (
                (dq_out, dq_hbm), (dk_out, dk_hbm), (dv_out, dv_hbm),
                (dqg_out, dqg_hbm), (dkg_out, dkg_hbm),
            )
        )
    ]
    totals = [ring_sum(half, 0) for half in (LOW, HIGH)]
    for first, pair in partial.items():
        for half in (LOW, HIGH):
            gain_part(half, first, pair[half][1] * SCALE)
    for half in (LOW, HIGH):
        gain_part(half, 0, totals[half][1] * SCALE)

    def gain_copy(slot):
        return pltpu.make_async_remote_copy(
            src_ref=gain_buf.at[0],
            dst_ref=gain_buf.at[slot],
            send_sem=sent.at[5],
            recv_sem=small_sem.at[1],
            device_id=to_ctx(ORDER[slot]),
            device_id_type=pl.DeviceIdType.MESH,
        )

    for slot in range(SLOTS - 1, 0, -1):
        gain_copy(slot).start()

    stat[2, 0] = jnp.zeros((8, SPAN), F32)
    for half in (LOW, HIGH):
        finished(gotp.at[half, pl.ds(1, 3)], ps_sem.at[half])
        total = totals[half]
        for first in (2, 1, 3):
            total = total + gotp[half, first].astype(F32)
        dkn[1, half] = total[0]
        d_norm = rotated(half, total[1] * SCALE, -1)
        k_hat = kv[half, 0, KEY].astype(F32) * ki[half]
        scaled = d_norm * k_gain_row()
        dkn[0, half] = scaled
        stat[2, 0, half:half + 1, :] = token_sums(scaled * k_hat)
    stat_send(2)

    for place, half in places:
        dv_out[place * SPAN:(place + 1) * SPAN, :] = dkn[1, half].astype(BF16)
    stores[2].start()

    q_inner = stat_total(1) / D
    for half in (LOW, HIGH):
        inner = spread(q_inner[half:half + 1, :])
        for h in range(GROUP):
            q_hat = q_ref[offs[half], :, head(h)].astype(F32) * qi[half]
            sg[half, :, head(h)] = qi[half] * (sg[half, :, head(h)] - q_hat * inner)

    for place, half in places:
        dq_out[place * SPAN:(place + 1) * SPAN, :] = sg[half].astype(BF16)
    stores[0].start()

    k_inner = stat_total(2) / KVD
    for half in (LOW, HIGH):
        inner = spread(k_inner[half:half + 1, :])
        k_hat = kv[half, 0, KEY].astype(F32) * ki[half]
        dkn[0, half] = ki[half] * (dkn[0, half] - k_hat * inner)
    for place, half in places:
        dk_out[place * SPAN:(place + 1) * SPAN, :] = dkn[0, half].astype(BF16)
    stores[1].start()

    finished(gain_buf.at[pl.ds(1, SLOTS - 1)], small_sem.at[1])
    total = gain_buf[0]
    for slot in range(1, SLOTS):
        total = total + gain_buf[slot]
    for h in range(GROUP):
        dqg_out[head(h)] = total[h:h + 1, :].reshape(DH)
    dkg_out[...] = total[5:6, :].reshape(DH)
    stores[3].start()
    stores[4].start()

    finished(kv.at[:, pl.ds(0, SLOTS - 1)], sent.at[0])
    finished(stage.at[:, :, pl.ds(1, 3)], sent.at[1])
    finished(pstage.at[:, pl.ds(1, 3)], sent.at[2])
    finished(stat.at[:, pl.ds(1, 7)], sent.at[3])
    finished(inv_buf.at[pl.ds(1, SLOTS - 1)], sent.at[4])
    finished(gain_buf.at[pl.ds(1, SLOTS - 1)], sent.at[5])
    for item in stores:
        item.wait()


def pass_on(*refs):
    for source, target in zip(refs[:5], refs[5:]):
        target[...] = source[...]


def per_device(q_raw, k_raw, values, d_out, q_gain, k_gain, span_order):
    token_table, span_table = tables()
    tile = (SPAN, DH)
    dma = pltpu.SemaphoreType.DMA
    wide = (SPAN, QW)
    scratch = [
        pltpu.SMEM((SPANS,), jnp.int32),
        pltpu.VMEM((QW,), F32), pltpu.VMEM((DH,), F32),
        pltpu.VMEM((2,) + tile, F32), pltpu.VMEM((2, SPANS, 1, DH), F32),
        pltpu.VMEM((2 * SPAN, QW), BF16), pltpu.VMEM((2 * SPAN, DH), BF16),
        pltpu.VMEM((2 * SPAN, DH), BF16), pltpu.VMEM((QW,), F32), pltpu.VMEM((DH,), F32),
        pltpu.SMEM((SLOTS,), jnp.int32),
        pltpu.SMEM((SLOTS,), jnp.int32),
        pltpu.VMEM((2,) + wide, BF16),
        pltpu.VMEM((2,) + tile, BF16),
        pltpu.VMEM((2,) + tile, BF16),
        pltpu.VMEM((2,) + wide, BF16),
        pltpu.VMEM((2, SLOTS, 2) + tile, BF16),
        pltpu.VMEM((2, SLOTS) + tile, BF16),
        pltpu.VMEM((2, QW, DH), BF16),
        pltpu.VMEM((2, DH, QW), BF16),
        pltpu.VMEM((2, QW, DH), BF16),
        pltpu.VMEM((2, DH, QW), BF16),
        pltpu.VMEM((2, 2) + tile, F32),
        pltpu.VMEM((2,) + tile, F32),
        pltpu.VMEM((2,) + tile, F32),
        pltpu.VMEM((16,) + wide, F32),
        pltpu.VMEM((17,) + wide, F32),
        pltpu.VMEM((16,) + wide, F32),
        pltpu.VMEM((17,) + wide, F32),
        pltpu.VMEM((32, 1, QW), F32),
        pltpu.VMEM((32, 1, QW), F32),
        pltpu.VMEM((32, 1, QW), F32),
        pltpu.VMEM((16, 1, QW), F32),
        pltpu.VMEM((16, 1, QW), F32),
        pltpu.VMEM((16, 1, QW), F32),
        pltpu.VMEM((32, 1, QW), F32),
        pltpu.VMEM((16, 1, QW), F32),
        pltpu.VMEM((2, 1, QW), F32),
        pltpu.VMEM((3,) + wide, BF16),
        pltpu.VMEM((3 * SPAN, QW), BF16),
        pltpu.VMEM((2,) + wide, F32),
        pltpu.VMEM((SLOTS, 2, 2) + tile, F32),
        pltpu.VMEM((2, RING, RING, 2) + tile, BF16),
        pltpu.VMEM((2, RING, RING, 2) + tile, BF16),
        pltpu.VMEM((2, RING, 2) + tile, BF16),
        pltpu.VMEM((2, RING, 2) + tile, BF16),
        pltpu.VMEM((2,) + wide, F32),
        pltpu.VMEM((2, 2) + tile, F32),
        pltpu.VMEM((3, 8, 8, SPAN), F32),
        pltpu.VMEM((SLOTS, 8, SPAN), F32),
        pltpu.VMEM((SLOTS, 8, DH), F32),
        dma((9,)), dma((5,)), pltpu.SemaphoreType.REGULAR,
        dma((6,)),
        dma((2, 10)), dma((2,)),
        dma((2, RING)), dma((2, RING)),
        dma((2,)), dma((3,)), dma((2,)),
    ]
    rows = 2 * SPAN
    shapes = (
        jax.ShapeDtypeStruct((rows, QW), BF16),
        jax.ShapeDtypeStruct((rows, DH), BF16),
        jax.ShapeDtypeStruct((rows, DH), BF16),
        jax.ShapeDtypeStruct((QW,), F32),
        jax.ShapeDtypeStruct((DH,), F32),
    )
    vmem = pl.BlockSpec(memory_space=pltpu.VMEM)
    hbm = pl.BlockSpec(memory_space=pltpu.HBM)
    results = pl.pallas_call(
        kernel,
        out_shape=shapes,
        in_specs=[hbm] * 9,
        out_specs=(hbm,) * 5,
        scratch_shapes=scratch,
        compiler_params=pltpu.CompilerParams(
            collective_id=0, has_side_effects=True, vmem_limit_bytes=60 * 2**20
        ),
    )(
        span_order,
        q_raw.reshape(2, SPAN, QW), k_raw.reshape(2, SPAN, DH),
        values.reshape(2, SPAN, DH), d_out.reshape(2, SPAN, QW),
        q_gain, k_gain, token_table, span_table,
    )
    return pl.pallas_call(
        pass_on, out_shape=shapes, in_specs=[vmem] * 5, out_specs=(vmem,) * 5,
        compiler_params=pltpu.CompilerParams(vmem_limit_bytes=60 * 2**20),
    )(*results)


def solution(mesh):
    return jax.shard_map(
        per_device,
        mesh=mesh,
        in_specs=(
            P("ctx", "tp"),
            P("ctx", "tp"),
            P("ctx", "tp"),
            P("ctx", "tp"),
            P("tp"),
            P("tp"),
            P(),
        ),
        out_specs=(P("ctx", "tp"), P("ctx", "tp"), P("ctx", "tp"), P("tp"), P("tp")),
        check_vma=False,
    )
```

```python
import math

import jax
import jax.numpy as jnp
import numpy as np
from jax import lax
from jax.experimental import pallas as pl
from jax.experimental.pallas import tpu as pltpu
from jax.sharding import PartitionSpec as P

D = 5120
KVD = 1024
DH = 128
SPAN = 128
SPANS = 32
GROUP = 5
QW = GROUP * DH
EPS = 1e-06
THETA = 500000.0
NEG = -1e30
SCALE = DH ** (-0.5)
C2 = SCALE * math.log2(math.e)
RING = 4
SLOTS = 16
F32 = jnp.float32
BF16 = jnp.bfloat16

ORDER = [
    (0, 0), (0, 3), (3, 0), (0, 1), (1, 0), (0, 2), (2, 0), (3, 3),
    (1, 3), (3, 1), (1, 1), (3, 2), (2, 3), (1, 2), (2, 1), (2, 2),
]
SLOT = {pair: number for number, pair in enumerate(ORDER)}
MIRROR = [SLOT[(-oz % RING, -ox % RING)] for oz, ox in ORDER]
RINGS = [(0, 1), (0, 2), (0, 3), (1, 0), (2, 0), (3, 0)]
CHUNKS = ((0, 256), (256, 256), (512, 128))
LOW, HIGH = 0, 1
KEY, VAL = 0, 1


def primary_view(half, slot):
    oz, ox = ORDER[slot]
    return (ox, oz) if half == LOW else (oz, ox)


def slot_of(half, first, second):
    return SLOT[(second, first)] if half == LOW else SLOT[(first, second)]


def gather_sends(half, slot):
    first, second = primary_view(half, slot)
    sends = []
    if second == 0:
        if first == 0:
            sends += [(0, step, slot_of(half, -step % RING, 0)) for step in (1, 3, 2)]
        sends += [(1, step, slot_of(half, first, -step % RING)) for step in (1, 3)]
        if first == 2:
            sends += [(1, 2, slot_of(half, first, 2))]
    if second == 3 and first != 2:
        sends += [(1, 1, slot_of(half, first, 2))]
    return sends


def tables():
    freq = np.asarray(
        np.float32(THETA) ** (-np.arange(DH // 2, dtype=np.float32) / np.float32(DH // 2)),
        np.float64,
    )
    sign = np.concatenate([-np.ones(DH // 2), np.ones(DH // 2)])

    def pair(numbers):
        angle = np.asarray(numbers, np.float64)[:, None] * freq[None, :]
        cos = np.concatenate([np.cos(angle)] * 2, axis=1)
        sin = np.concatenate([np.sin(angle)] * 2, axis=1) * sign
        return cos, sin

    cos_t, sin_t = pair(np.arange(SPAN))
    cos_s, sin_s = pair(np.arange(SPANS) * SPAN)
    token = np.stack([cos_t, sin_t]).astype(np.float32)
    span = np.stack([cos_s, sin_s])[:, :, None, :].astype(np.float32)
    return jnp.asarray(token), jnp.asarray(span)


def kernel(
    so_in, q_in, k_in, v_in, do_in, qg_in, kg_in, tab_in, span_in,
    dq_hbm, dk_hbm, dv_hbm, dqg_hbm, dkg_hbm,
    so_ref, qg_ref, kg_ref, tab_ref, span_ref, dq_out, dk_out, dv_out, dqg_out, dkg_out,
    sel_ref, low_ref, q_ref, k_ref, v_ref, do_ref,
    kv, kr, qs, qt, dos, dot_, rope, qi, ki,
    e_a, e_b, dp_a, dp_b, mh, lh, dh, ml, ll, dl, fh, fl, delta,
    pb, dsb, acc, cb, stage, gotr, pstage, gotp, sg, dkn,
    stat, inv_buf, gain_buf,
    in_sem, out_sem, relay, sent, ag_sem, rest_sem, far_sem, rs_sem, ps_sem, st_sem, small_sem,
):
    order_load = pltpu.make_async_copy(so_in, so_ref, in_sem.at[8])
    order_load.start()
    loads = [
        pltpu.make_async_copy(source, target, in_sem.at[number])
        for number, (source, target) in enumerate(
            (
                (k_in, k_ref), (v_in, v_ref), (q_in, q_ref), (do_in, do_ref),
                (qg_in, qg_ref), (kg_in, kg_ref), (tab_in, tab_ref), (span_in, span_ref),
            )
        )
    ]
    for load in loads:
        load.start()

    ctx = lax.axis_index("ctx")
    tp = lax.axis_index("tp")
    z, x = ctx // RING, ctx % RING
    flip = tp % 2
    turned_z = [z] + [(z + jnp.where(flip == 0, o, RING - o)) % RING for o in (1, 2, 3)]
    turned_x = [x] + [(x + jnp.where(flip == 0, o, RING - o)) % RING for o in (1, 2, 3)]
    peers = {(oz, ox): turned_z[oz] * RING + turned_x[ox] for oz, ox in ORDER}
    tp_peers = [(tp + offset) % 8 for offset in range(8)]

    def to_ctx(pair):
        return {"ctx": peers[pair]}

    barrier = pltpu.get_barrier_semaphore()
    for pair in RINGS:
        pl.semaphore_signal(
            barrier, inc=1, device_id=to_ctx(pair), device_id_type=pl.DeviceIdType.MESH
        )
    for offset in range(1, 8):
        pl.semaphore_signal(
            barrier, inc=1, device_id={"tp": tp_peers[offset]},
            device_id_type=pl.DeviceIdType.MESH,
        )

    order_load.wait()
    s0, s1 = so_ref[2 * ctx], so_ref[2 * ctx + 1]
    low = jnp.minimum(s0, s1)
    offs = (jnp.where(s0 < s1, 0, 1), jnp.where(s0 < s1, 1, 0))
    low_ref[0] = low
    for slot in range(1, SLOTS):
        other = peers[ORDER[slot]]
        a = jnp.minimum(so_ref[2 * other], so_ref[2 * other + 1])
        low_ref[slot] = a
        sel_ref[slot] = jnp.where(a < low, 1, 0)

    loads[0].wait()
    loads[1].wait()
    for half in (LOW, HIGH):
        kv[half, 0, KEY] = k_ref[offs[half]]
        kv[half, 0, VAL] = v_ref[offs[half]]

    pl.semaphore_wait(barrier, 13)

    axis_of = {LOW: ("x", "z"), HIGH: ("z", "x")}

    def neighbour(half, axis, step):
        return to_ctx((step, 0) if axis_of[half][axis] == "z" else (0, step))

    def gather_arrival(half, dst):
        if dst < 10:
            return ag_sem.at[half, dst]
        return rest_sem.at[0 if dst < 13 else 1]

    def gather_copy(half, slot, axis, step, dst):
        return pltpu.make_async_remote_copy(
            src_ref=kv.at[half, slot],
            dst_ref=kv.at[half, dst],
            send_sem=sent.at[0],
            recv_sem=gather_arrival(half, dst),
            device_id=neighbour(half, axis, step),
            device_id_type=pl.DeviceIdType.MESH,
        )

    def gather_forward(half, slot):
        for axis, step, dst in gather_sends(half, slot):
            gather_copy(half, slot, axis, step, dst).start()

    def hop(slots):
        for slot in slots:
            for half in (LOW, HIGH):
                gather_copy(half, slot, 0, 1, slot).wait_recv()
                gather_forward(half, slot)

    def finished(block, sem):
        pltpu.make_async_copy(block, block, sem).wait()

    def rest(first):
        finished(kv.at[:, pl.ds(first, 3)], rest_sem.at[0 if first < 13 else 1])

    gather_forward(LOW, 0)
    gather_forward(HIGH, 0)
    for pair in RINGS[3:]:
        pl.semaphore_signal(
            relay, inc=1, device_id=to_ctx(pair), device_id_type=pl.DeviceIdType.MESH
        )

    def stat_copy(kind, offset):
        return pltpu.make_async_remote_copy(
            src_ref=stat.at[kind, 0],
            dst_ref=stat.at[kind, offset],
            send_sem=sent.at[3],
            recv_sem=st_sem.at[kind],
            device_id={"tp": tp_peers[offset]},
            device_id_type=pl.DeviceIdType.MESH,
        )

    def stat_send(kind):
        for offset in range(1, 8):
            stat_copy(kind, offset).start()

    def stat_total(kind):
        finished(stat.at[kind, pl.ds(1, 7)], st_sem.at[kind])
        total = stat[kind, 0]
        for offset in range(1, 8):
            total = total + stat[kind, offset]
        return total

    def token_sums(square):
        return jnp.sum(jnp.transpose(square), axis=0, keepdims=True)

    def spread(row):
        return jnp.transpose(jnp.broadcast_to(row, (SPAN, SPAN)))

    def head(number):
        return slice(number * DH, (number + 1) * DH)

    def q_gain_row(h):
        return qg_ref[head(h)].reshape(1, DH)

    def k_gain_row():
        return kg_ref[...].reshape(1, DH)

    for load in loads[2:]:
        load.wait()
    stat[0, 0] = jnp.zeros((8, SPAN), F32)
    for half in (LOW, HIGH):
        square = jnp.zeros((SPAN, DH), F32)
        for h in range(GROUP):
            part = q_ref[offs[half], :, head(h)].astype(F32)
            square = square + part * part
        stat[0, 0, half:half + 1, :] = token_sums(square)
        part = kv[half, 0, KEY].astype(F32)
        stat[0, 0, 2 + half:3 + half, :] = token_sums(part * part)
    stat_send(0)

    def rope_tables(span):
        cos_t, sin_t = tab_ref[0], tab_ref[1]
        cos_s, sin_s = span_ref[0, span], span_ref[1, span]
        return cos_s * cos_t - sin_s * sin_t, sin_s * cos_t + cos_s * sin_t

    for half, span in ((LOW, low), (HIGH, SPANS - 1 - low)):
        rope[half, 0], rope[half, 1] = rope_tables(span)
    for half in (LOW, HIGH):
        for h in range(GROUP):
            part = do_ref[offs[half], :, head(h)]
            dos[half, head(h), :] = part
            dot_[half, :, head(h)] = jnp.transpose(part)

    def rotated(half, part, sign):
        turned = pltpu.roll(part, DH // 2, 1) * rope[half, 1]
        straight = part * rope[half, 0]
        return straight + turned if sign > 0 else straight - turned

    total = stat_total(0)
    pl.semaphore_wait(relay, 3)
    inv_buf[0] = lax.rsqrt(total / KVD + EPS)
    q_inv = lax.rsqrt(total / D + EPS)

    def inv_copy(slot):
        return pltpu.make_async_remote_copy(
            src_ref=inv_buf.at[0],
            dst_ref=inv_buf.at[MIRROR[slot]],
            send_sem=sent.at[4],
            recv_sem=small_sem.at[0],
            device_id=to_ctx(ORDER[slot]),
            device_id_type=pl.DeviceIdType.MESH,
        )

    for slot in range(1, SLOTS):
        inv_copy(slot).start()

    hop((1, 2, 3, 4))

    for half in (LOW, HIGH):
        ki[half] = spread(inv_buf[0, 2 + half:3 + half, :])
        part = kv[half, 0, KEY].astype(F32) * ki[half] * k_gain_row()
        kr[half, 0] = rotated(half, part, 1).astype(BF16)
        qi[half] = spread(q_inv[half:half + 1, :])
        for h in range(GROUP):
            part = q_ref[offs[half], :, head(h)].astype(F32) * qi[half] * q_gain_row(h)
            turned = rotated(half, part, 1).astype(BF16)
            qs[half, head(h), :] = turned
            qt[half, :, head(h)] = jnp.transpose(turned)

    hop((5, 6))

    def mm(a, b):
        return jnp.dot(a, b, preferred_element_type=F32)

    def pick(is_low, low_rows, high_rows):
        return jnp.where(is_low, low_rows, high_rows)

    def key_rows(half, slot):
        span = low_ref[slot] if half == LOW else SPANS - 1 - low_ref[slot]
        cos, sin = rope_tables(span)
        part = kv[half, slot, KEY].astype(F32)
        part = part * spread(inv_buf[slot, 2 + half:3 + half, :]) * k_gain_row()
        part = part * cos + pltpu.roll(part, DH // 2, 1) * sin
        kr[half, slot] = part.astype(BF16)

    def values_pass(slot):
        is_low = sel_ref[slot] == 1
        other = 1 - sel_ref[slot]
        v_low = kv[LOW, slot, VAL]
        v_other = pick(is_low, v_low, kv[HIGH, slot, VAL])
        for start, width in CHUNKS:
            cols = pl.ds(start, width)
            dp_a[slot, :, cols] = mm(v_low, dot_[HIGH, :, cols])
            dp_b[slot, :, cols] = mm(v_other, dot_[other, :, cols])

    def scores(keys, half, cols, d_probs, exps, slot, mask=None):
        s = mm(keys, qt[half, :, cols])
        if mask is not None:
            s = jnp.where(mask, s, NEG)
        top = jnp.max(s, axis=0, keepdims=True)
        e = jnp.exp2(s * C2 - top * C2)
        exps[slot, :, cols] = e
        return (
            top,
            jnp.sum(e, axis=0, keepdims=True),
            jnp.sum(e * d_probs[slot, :, cols], axis=0, keepdims=True),
        )

    def put(tabs, row, cols, stats):
        for tab, value in zip(tabs, stats):
            tab[row, :, cols] = value

    tabs_high, tabs_low = (mh, lh, dh), (ml, ll, dl)

    def keys_pass(slot):
        chosen = sel_ref[slot]
        is_low = chosen == 1
        for half in (LOW, HIGH):
            key_rows(half, slot)
        k_low = kr[LOW, slot]
        k_other = pick(is_low, k_low, kr[HIGH, slot])
        for start, width in CHUNKS:
            cols = pl.ds(start, width)
            put(tabs_high, slot, cols, scores(k_low, HIGH, cols, dp_a, e_a, slot))
            top, total, dots = scores(k_other, 1 - chosen, cols, dp_b, e_b, slot)
            put(tabs_high, slot + 15, cols, (jnp.where(is_low, NEG, top), total, dots))
            put(tabs_low, slot, cols, (jnp.where(is_low, top, NEG), total, dots))

    def own_values():
        for start, width in CHUNKS:
            cols = pl.ds(start, width)
            dp_a[0, :, cols] = mm(kv[LOW, 0, VAL], dot_[HIGH, :, cols])
            dp_b[0, :, cols] = mm(kv[LOW, 0, VAL], dot_[LOW, :, cols])
            dp_b[16, :, cols] = mm(kv[HIGH, 0, VAL], dot_[HIGH, :, cols])

    def own_keys():
        for start, width in CHUNKS:
            cols = pl.ds(start, width)
            shape = (SPAN, width)
            mask = lax.broadcasted_iota(jnp.int32, shape, 0) <= (
                lax.broadcasted_iota(jnp.int32, shape, 1) % SPAN
            )
            put(tabs_high, 0, cols, scores(kr[LOW, 0], HIGH, cols, dp_a, e_a, 0))
            put(tabs_low, 0, cols, scores(kr[LOW, 0], LOW, cols, dp_b, e_b, 0, mask))
            put(tabs_high, 31, cols, scores(kr[HIGH, 0], HIGH, cols, dp_b, e_b, 16, mask))

    def each(step, slots):
        for slot in slots:
            step(slot)

    own_values()
    own_keys()
    each(values_pass, (1, 2, 3, 4))
    hop((7, 8, 9))
    each(values_pass, (5, 6))
    finished(inv_buf.at[pl.ds(1, SLOTS - 1)], small_sem.at[0])
    each(keys_pass, (1, 2, 3, 4, 5, 6))
    rest(10)
    each(values_pass, (7, 8, 9, 10, 11, 12))
    each(keys_pass, (7, 8, 9, 10, 11, 12))
    rest(13)
    each(values_pass, (13, 14, 15))
    each(keys_pass, (13, 14, 15))

    def finish(tabs, factors, half):
        tops, sums, dots = (tab[...] for tab in tabs)
        weights = jnp.exp2((tops - jnp.max(tops, axis=0, keepdims=True)) * C2)
        scale = 1.0 / jnp.sum(weights * sums, axis=0, keepdims=True)
        delta[half] = (jnp.sum(weights * dots, axis=0, keepdims=True) * scale)[0]
        factors[...] = weights * scale

    finish(tabs_high, fh, HIGH)
    finish(tabs_low, fl, LOW)

    def grads(exps, d_probs, slot, factor, shift, where):
        for start, width in CHUNKS:
            cols = pl.ds(start, width)
            probs = exps[slot, :, cols] * factor(cols)
            d_scores = probs * (d_probs[slot, :, cols] - shift(cols))
            pb[where, :, cols] = probs.astype(BF16)
            dsb[pl.ds(where * SPAN, SPAN), cols] = d_scores.astype(BF16)

    def rows(where):
        return pl.ds(where * SPAN, SPAN)

    def second_pass(slot):
        chosen = sel_ref[slot]
        is_low = chosen == 1
        other = 1 - chosen
        grads(e_a, dp_a, slot, lambda c: fh[slot, :, c], lambda c: delta[HIGH, :, c], 0)
        grads(
            e_b, dp_b, slot,
            lambda c: fl[slot, :, c] + fh[slot + 15, :, c],
            lambda c: delta[other, :, c], 1,
        )
        for kind, left in ((0, None), (1, None)):
            a_rows = pb[0] if kind == 0 else dsb[rows(0), :]
            b_rows = pb[1] if kind == 0 else dsb[rows(1), :]
            source = dos if kind == 0 else qs
            from_a = mm(a_rows, source[HIGH])
            from_b = mm(b_rows, source[other])
            cb[slot, LOW, kind] = from_a + jnp.where(is_low, from_b, 0.0)
            cb[slot, HIGH, kind] = jnp.where(is_low, 0.0, from_b)
        turned_low = jnp.transpose(kr[LOW, slot])
        turned_other = jnp.transpose(pick(is_low, kr[LOW, slot], kr[HIGH, slot]))
        none = jnp.zeros_like(turned_other)
        both = jnp.concatenate([turned_low, jnp.where(is_low, none, turned_other)], axis=1)
        only_low = jnp.where(is_low, turned_other, none)
        for start, width in CHUNKS:
            cols = pl.ds(start, width)
            acc[HIGH, :, cols] += mm(both, dsb[0:2 * SPAN, cols])
            acc[LOW, :, cols] += mm(only_low, dsb[rows(1), cols])

    def own_second():
        grads(e_a, dp_a, 0, lambda c: fh[0, :, c], lambda c: delta[HIGH, :, c], 0)
        grads(e_b, dp_b, 16, lambda c: fh[31, :, c], lambda c: delta[HIGH, :, c], 1)
        grads(e_b, dp_b, 0, lambda c: fl[0, :, c], lambda c: delta[LOW, :, c], 2)
        for kind in (0, 1):
            source = dos if kind == 0 else qs
            parts = [pb[i] if kind == 0 else dsb[rows(i), :] for i in range(3)]
            cb[0, LOW, kind] = mm(parts[0], source[HIGH]) + mm(parts[2], source[LOW])
            cb[0, HIGH, kind] = mm(parts[1], source[HIGH])
        turned_low = jnp.transpose(kr[LOW, 0])
        turned_high = jnp.transpose(kr[HIGH, 0])
        both = jnp.concatenate([turned_low, turned_high], axis=1)
        for start, width in CHUNKS:
            cols = pl.ds(start, width)
            acc[HIGH, :, cols] += mm(both, dsb[0:2 * SPAN, cols])
            acc[LOW, :, cols] += mm(turned_low, dsb[rows(2), cols])

    acc[...] = jnp.zeros_like(acc)

    PLACE = {1: 1, 3: 2, 2: 3}

    def ring_copy(half, first, place):
        step = {1: 1, 2: 3, 3: 2 if first == 2 else 1}[place]
        return pltpu.make_async_remote_copy(
            src_ref=stage.at[half, first, place],
            dst_ref=gotr.at[half, first, place],
            send_sem=sent.at[1],
            recv_sem=(far_sem if first != 2 and place == 3 else rs_sem).at[half, first],
            device_id=neighbour(half, 1, step),
            device_id_type=pl.DeviceIdType.MESH,
        )

    def last_copy(half, first):
        return pltpu.make_async_remote_copy(
            src_ref=pstage.at[half, first],
            dst_ref=gotp.at[half, first],
            send_sem=sent.at[2],
            recv_sem=ps_sem.at[half],
            device_id=neighbour(half, 0, first),
            device_id_type=pl.DeviceIdType.MESH,
        )

    def ring_send(half, slot):
        first, second = primary_view(half, slot)
        if second > 1 or (second == 1 and first == 2):
            stage[half, first, PLACE[second]] = cb[slot, half].astype(BF16)
            ring_copy(half, first, PLACE[second]).start()

    def near_send(first):
        for half in (LOW, HIGH):
            ring_copy(half, first, 3).wait_recv()
            mixed = cb[slot_of(half, first, 1), half] + gotr[half, first, 3].astype(F32)
            stage[half, first, 1] = mixed.astype(BF16)
            ring_copy(half, first, 1).start()

    def ring_sum(half, first):
        count = 3 if first == 2 else 2
        finished(gotr.at[half, first, pl.ds(1, count)], rs_sem.at[half, first])
        total = cb[slot_of(half, first, 0), half]
        for place in range(1, count + 1):
            total = total + gotr[half, first, place].astype(F32)
        return total

    def gain_part(half, first, d_rot):
        slot = slot_of(half, first, 0)
        span = low_ref[slot] if half == LOW else SPANS - 1 - low_ref[slot]
        cos, sin = rope_tables(span)
        d_norm = d_rot * cos - pltpu.roll(d_rot, DH // 2, 1) * sin
        k_hat = kv[half, slot, KEY].astype(F32) * spread(inv_buf[slot, 2 + half:3 + half, :])
        gain_buf[0, 5:6, :] += jnp.sum(d_norm * k_hat, axis=0, keepdims=True)

    def last_send(first):
        totals = []
        for half in (LOW, HIGH):
            totals.append(ring_sum(half, first))
            pstage[half, first] = totals[half].astype(BF16)
            last_copy(half, first).start()
        return totals

    steps = (15, 14, 13, 12, 11, 7, 9, 8, 6, 5, 10, 4, 3, 2, 1)
    near = {4: 1, 2: 3}
    for slot in steps:
        second_pass(slot)
        for half in (LOW, HIGH):
            ring_send(half, slot)
        if slot in near:
            near_send(near[slot])
    own_second()
    partial = {2: last_send(2)}

    stat[1, 0] = jnp.zeros((8, SPAN), F32)
    gain_buf[0] = jnp.zeros((8, DH), F32)
    for half in (LOW, HIGH):
        inner = jnp.zeros((SPAN, DH), F32)
        for h in range(GROUP):
            d_rot = jnp.transpose(acc[half, :, head(h)]) * SCALE
            d_norm = rotated(half, d_rot, -1)
            q_hat = q_ref[offs[half], :, head(h)].astype(F32) * qi[half]
            gain_buf[0, h:h + 1, :] += jnp.sum(d_norm * q_hat, axis=0, keepdims=True)
            scaled = d_norm * q_gain_row(h)
            sg[half, :, head(h)] = scaled
            inner = inner + scaled * q_hat
        stat[1, 0, half:half + 1, :] = token_sums(inner)
    stat_send(1)

    near_send(0)
    for first in (1, 3):
        partial[first] = last_send(first)

    first_half = jnp.where(s0 < s1, LOW, HIGH)
    places = ((0, first_half), (1, 1 - first_half))
    def store(number, source, target):
        return pltpu.make_async_copy(source, target, out_sem.at[number])

    stores = [
        store(number, source, target)
        for number, (source, target) in enumerate(
            (
                (dq_out, dq_hbm), (dk_out, dk_hbm), (dv_out, dv_hbm),
                (dqg_out, dqg_hbm), (dkg_out, dkg_hbm),
            )
        )
    ]
    totals = [ring_sum(half, 0) for half in (LOW, HIGH)]
    for first, pair in partial.items():
        for half in (LOW, HIGH):
            gain_part(half, first, pair[half][1] * SCALE)
    for half in (LOW, HIGH):
        gain_part(half, 0, totals[half][1] * SCALE)

    def gain_copy(slot):
        return pltpu.make_async_remote_copy(
            src_ref=gain_buf.at[0],
            dst_ref=gain_buf.at[slot],
            send_sem=sent.at[5],
            recv_sem=small_sem.at[1],
            device_id=to_ctx(ORDER[slot]),
            device_id_type=pl.DeviceIdType.MESH,
        )

    for slot in range(SLOTS - 1, 0, -1):
        gain_copy(slot).start()

    stat[2, 0] = jnp.zeros((8, SPAN), F32)
    for half in (LOW, HIGH):
        finished(gotp.at[half, pl.ds(1, 3)], ps_sem.at[half])
        total = totals[half]
        for first in (2, 1, 3):
            total = total + gotp[half, first].astype(F32)
        dkn[1, half] = total[0]
        d_norm = rotated(half, total[1] * SCALE, -1)
        k_hat = kv[half, 0, KEY].astype(F32) * ki[half]
        scaled = d_norm * k_gain_row()
        dkn[0, half] = scaled
        stat[2, 0, half:half + 1, :] = token_sums(scaled * k_hat)
    stat_send(2)

    for place, half in places:
        dv_out[place * SPAN:(place + 1) * SPAN, :] = dkn[1, half].astype(BF16)
    stores[2].start()

    q_inner = stat_total(1) / D
    for half in (LOW, HIGH):
        inner = spread(q_inner[half:half + 1, :])
        for h in range(GROUP):
            q_hat = q_ref[offs[half], :, head(h)].astype(F32) * qi[half]
            sg[half, :, head(h)] = qi[half] * (sg[half, :, head(h)] - q_hat * inner)

    for place, half in places:
        dq_out[place * SPAN:(place + 1) * SPAN, :] = sg[half].astype(BF16)
    stores[0].start()

    finished(gain_buf.at[pl.ds(1, SLOTS - 1)], small_sem.at[1])
    total = gain_buf[0]
    for slot in range(1, SLOTS):
        total = total + gain_buf[slot]
    for h in range(GROUP):
        dqg_out[head(h)] = total[h:h + 1, :].reshape(DH)
    dkg_out[...] = total[5:6, :].reshape(DH)
    stores[3].start()
    stores[4].start()
    finished(kv.at[:, pl.ds(0, SLOTS - 1)], sent.at[0])
    finished(stage.at[:, :, pl.ds(1, 3)], sent.at[1])
    finished(pstage.at[:, pl.ds(1, 3)], sent.at[2])
    finished(inv_buf.at[pl.ds(1, SLOTS - 1)], sent.at[4])
    finished(gain_buf.at[pl.ds(1, SLOTS - 1)], sent.at[5])

    k_inner = stat_total(2) / KVD
    for half in (LOW, HIGH):
        inner = spread(k_inner[half:half + 1, :])
        k_hat = kv[half, 0, KEY].astype(F32) * ki[half]
        dkn[0, half] = ki[half] * (dkn[0, half] - k_hat * inner)
    for place, half in places:
        dk_out[place * SPAN:(place + 1) * SPAN, :] = dkn[0, half].astype(BF16)
    stores[1].start()

    finished(stat.at[:, pl.ds(1, 7)], sent.at[3])
    for item in stores:
        item.wait()


def pass_on(*refs):
    for source, target in zip(refs[:5], refs[5:]):
        target[...] = source[...]


def per_device(q_raw, k_raw, values, d_out, q_gain, k_gain, span_order):
    token_table, span_table = tables()
    tile = (SPAN, DH)
    dma = pltpu.SemaphoreType.DMA
    wide = (SPAN, QW)
    scratch = [
        pltpu.SMEM((SPANS,), jnp.int32),
        pltpu.VMEM((QW,), F32), pltpu.VMEM((DH,), F32),
        pltpu.VMEM((2,) + tile, F32), pltpu.VMEM((2, SPANS, 1, DH), F32),
        pltpu.VMEM((2 * SPAN, QW), BF16), pltpu.VMEM((2 * SPAN, DH), BF16),
        pltpu.VMEM((2 * SPAN, DH), BF16), pltpu.VMEM((QW,), F32), pltpu.VMEM((DH,), F32),
        pltpu.SMEM((SLOTS,), jnp.int32),
        pltpu.SMEM((SLOTS,), jnp.int32),
        pltpu.VMEM((2,) + wide, BF16),
        pltpu.VMEM((2,) + tile, BF16),
        pltpu.VMEM((2,) + tile, BF16),
        pltpu.VMEM((2,) + wide, BF16),
        pltpu.VMEM((2, SLOTS, 2) + tile, BF16),
        pltpu.VMEM((2, SLOTS) + tile, BF16),
        pltpu.VMEM((2, QW, DH), BF16),
        pltpu.VMEM((2, DH, QW), BF16),
        pltpu.VMEM((2, QW, DH), BF16),
        pltpu.VMEM((2, DH, QW), BF16),
        pltpu.VMEM((2, 2) + tile, F32),
        pltpu.VMEM((2,) + tile, F32),
        pltpu.VMEM((2,) + tile, F32),
        pltpu.VMEM((16,) + wide, F32),
        pltpu.VMEM((17,) + wide, F32),
        pltpu.VMEM((16,) + wide, F32),
        pltpu.VMEM((17,) + wide, F32),
        pltpu.VMEM((32, 1, QW), F32),
        pltpu.VMEM((32, 1, QW), F32),
        pltpu.VMEM((32, 1, QW), F32),
        pltpu.VMEM((16, 1, QW), F32),
        pltpu.VMEM((16, 1, QW), F32),
        pltpu.VMEM((16, 1, QW), F32),
        pltpu.VMEM((32, 1, QW), F32),
        pltpu.VMEM((16, 1, QW), F32),
        pltpu.VMEM((2, 1, QW), F32),
        pltpu.VMEM((3,) + wide, BF16),
        pltpu.VMEM((3 * SPAN, QW), BF16),
        pltpu.VMEM((2,) + wide, F32),
        pltpu.VMEM((SLOTS, 2, 2) + tile, F32),
        pltpu.VMEM((2, RING, RING, 2) + tile, BF16),
        pltpu.VMEM((2, RING, RING, 2) + tile, BF16),
        pltpu.VMEM((2, RING, 2) + tile, BF16),
        pltpu.VMEM((2, RING, 2) + tile, BF16),
        pltpu.VMEM((2,) + wide, F32),
        pltpu.VMEM((2, 2) + tile, F32),
        pltpu.VMEM((3, 8, 8, SPAN), F32),
        pltpu.VMEM((SLOTS, 8, SPAN), F32),
        pltpu.VMEM((SLOTS, 8, DH), F32),
        dma((9,)), dma((5,)), pltpu.SemaphoreType.REGULAR,
        dma((6,)),
        dma((2, 10)), dma((2,)),
        dma((2, RING)), dma((2, RING)),
        dma((2,)), dma((3,)), dma((2,)),
    ]
    rows = 2 * SPAN
    shapes = (
        jax.ShapeDtypeStruct((rows, QW), BF16),
        jax.ShapeDtypeStruct((rows, DH), BF16),
        jax.ShapeDtypeStruct((rows, DH), BF16),
        jax.ShapeDtypeStruct((QW,), F32),
        jax.ShapeDtypeStruct((DH,), F32),
    )
    vmem = pl.BlockSpec(memory_space=pltpu.VMEM)
    hbm = pl.BlockSpec(memory_space=pltpu.HBM)
    results = pl.pallas_call(
        kernel,
        out_shape=shapes,
        in_specs=[hbm] * 9,
        out_specs=(hbm,) * 5,
        scratch_shapes=scratch,
        compiler_params=pltpu.CompilerParams(
            collective_id=0, has_side_effects=True, vmem_limit_bytes=60 * 2**20
        ),
    )(
        span_order,
        q_raw.reshape(2, SPAN, QW), k_raw.reshape(2, SPAN, DH),
        values.reshape(2, SPAN, DH), d_out.reshape(2, SPAN, QW),
        q_gain, k_gain, token_table, span_table,
    )
    return pl.pallas_call(
        pass_on, out_shape=shapes, in_specs=[vmem] * 5, out_specs=(vmem,) * 5,
        compiler_params=pltpu.CompilerParams(vmem_limit_bytes=60 * 2**20),
    )(*results)


def solution(mesh):
    return jax.shard_map(
        per_device,
        mesh=mesh,
        in_specs=(
            P("ctx", "tp"),
            P("ctx", "tp"),
            P("ctx", "tp"),
            P("ctx", "tp"),
            P("tp"),
            P("tp"),
            P(),
        ),
        out_specs=(P("ctx", "tp"), P("ctx", "tp"), P("ctx", "tp"), P("tp"), P("tp")),
        check_vma=False,
    )
```
